32 devices in a mesh: grp: 2 (over core), gx: 4 (over y, x), gy: 4 (over z).
Axes of the slice: x: 2, y: 2, z: 4, core: 2. Of those that a mesh axis runs over, the one named last changes fastest.
Arguments:
- right_side: float32 [64, 64, 256], P('gx', 'gy', 'grp'), may hold values from -6 to 6
- coefficient: float32 [64, 64, 256], P('gx', 'gy', 'grp'), may hold values from 0.2 to 5
Outputs:
- solution_field: float32 [64, 64, 256], P('gx', 'gy', 'grp')
- residual: float32 [64, 64, 256], P('gx', 'gy', 'grp')
The draws below stay inside these ranges and needn't reach their ends.
All inputs are finite; a program needn't handle non-finite values.
Results may differ from the reference program's by a relative error of at most 0.0001.
Values sent between devices are 32-bit elements; how exact they have to be, the bound alone decides.
A program may use at most 64 MiB of HBM per device.

```python
import math
import jax
import jax.numpy as jnp

FINE_DEGREE = 5
COARSE_DEGREE = 16
OUTER = 2
NX = 64
NY = 64
NZ = 256


def block_levels(rng, dims, split, smallest, top_value):
    def one(position, blocks):
        heights = jax.random.uniform(jax.random.fold_in(jax.random.fold_in(rng, 6), position), (blocks,), jnp.float32, smallest / len(split), top_value / len(split))
        return jnp.repeat(jnp.exp(heights), dims[position] // blocks).reshape((-1,) + (1,) * (len(dims) - position - 1))

    gain = one(*split[0])
    for cut in split[1:]:
        gain = gain * one(*cut)
    return gain


def noise(key, shape, width, limit, split=(), held_as=jnp.bfloat16):
    loudness = block_levels(key, shape, split, -0.22, 0.18) if split else 1.0
    result = jax.random.normal(key, shape, jnp.float32) * width * loudness
    return jnp.minimum(jnp.maximum(result, -limit), limit).astype(held_as)


def setup_inputs(seed: int = 0) -> dict:
    key_of = jax.random.split(jax.random.key(seed), 3)
    right_side = noise(key_of[0], (NX, NY, NZ), 1.0, 6.0, ((0, 4), (1, 4), (2, 2)), jnp.float32)
    coefficient = jnp.clip(jnp.exp(math.log(5.0) - 3.218876 * jax.random.uniform(key_of[1], (NX, NY, NZ), jnp.float32) ** block_levels(key_of[1], (NX, NY, NZ), ((0, 4), (1, 4), (2, 2)), -0.2, 0.2)), 0.2, 5.0)
    return dict(right_side=right_side, coefficient=coefficient)


LOW_FINE = 0.2
LOW_COARSE = 0.02
HIGH_BOUND = 2.0
DAMPING = 0.5


def face_parts(padded):
    center = padded[1:-1, 1:-1, 1:-1]
    return (0.5 * (center + padded[:-2, 1:-1, 1:-1]), 0.5 * (center + padded[2:, 1:-1, 1:-1]),
            0.5 * (center + padded[1:-1, :-2, 1:-1]), 0.5 * (center + padded[1:-1, 2:, 1:-1]),
            0.5 * (center + padded[1:-1, 1:-1, :-2]), 0.5 * (center + padded[1:-1, 1:-1, 2:]))


def diagonal_of(parts):
    return parts[0] + parts[1] + parts[2] + parts[3] + parts[4] + parts[5]


def stencil(padded, parts, scale):
    center = padded[1:-1, 1:-1, 1:-1]
    nearby = parts[0] * padded[:-2, 1:-1, 1:-1] + parts[1] * padded[2:, 1:-1, 1:-1]
    nearby = nearby + parts[2] * padded[1:-1, :-2, 1:-1] + parts[3] * padded[1:-1, 2:, 1:-1]
    nearby = nearby + parts[4] * padded[1:-1, 1:-1, :-2] + parts[5] * padded[1:-1, 1:-1, 2:]
    return scale * (diagonal_of(parts) * center - nearby)


def restrict(field):
    size_a, size_b, size_c = field.shape
    return field.reshape(size_a // 2, 2, size_b // 2, 2, size_c // 2, 2).mean(axis=(1, 3, 5))


def prolong(field):
    return jnp.repeat(jnp.repeat(jnp.repeat(field, 2, 0), 2, 1), 2, 2)


def cheb_steps(degree, low, high):
    theta = (high + low) / 2.0
    delta = (high - low) / 2.0
    sigma = theta / delta
    rho = 1.0 / sigma
    keeps = []
    pushes = []
    for step in range(degree - 1):
        rho_new = 1.0 / (2.0 * sigma - rho)
        keeps.append(rho_new * rho)
        pushes.append(2.0 * rho_new / delta)
        rho = rho_new
    return 1.0 / theta, keeps, pushes


def chebyshev(rhs, inverse_diag, apply_fn, degree, low, high):
    inv_theta, keeps, pushes = cheb_steps(degree, low, high)
    first = inverse_diag * rhs * inv_theta
    resid, update, total = rhs, first, first
    for step in range(degree - 1):
        resid = resid - apply_fn(update)
        update = keeps[step] * update + pushes[step] * (inverse_diag * resid)
        total = total + update
    return total


def reference(right_side, coefficient):
    coefs = [coefficient]
    for level in range(3):
        coefs.append(restrict(coefs[-1]))
    scales = [1.0, 0.25, 0.0625, 0.015625]
    parts_all = [face_parts(jnp.pad(item, 1)) for item in coefs]
    inverses = [1.0 / (scales[level] * diagonal_of(parts_all[level])) for level in range(4)]

    def make_apply(level):
        return lambda field: stencil(jnp.pad(field, 1), parts_all[level], scales[level])

    solution_field = jnp.zeros_like(right_side)
    residual = right_side
    for outer in range(OUTER):
        rhs_list = [residual]
        for level in range(3):
            rhs_list.append(restrict(rhs_list[-1]))
        corrections = []
        for level in range(4):
            if level < 3:
                corrections.append(chebyshev(rhs_list[level], inverses[level], make_apply(level), FINE_DEGREE, LOW_FINE, HIGH_BOUND))
            else:
                corrections.append(chebyshev(rhs_list[level], inverses[level], make_apply(level), COARSE_DEGREE, LOW_COARSE, HIGH_BOUND))
        combined = corrections[2] + prolong(corrections[3])
        combined = corrections[1] + prolong(combined)
        combined = corrections[0] + prolong(combined)
        solution_field = solution_field + DAMPING * combined
        residual = right_side - stencil(jnp.pad(solution_field, 1), parts_all[0], 1.0)
    return solution_field, residual
```

```python
import functools

import jax
import jax.numpy as jnp
from jax import lax
from jax.experimental import pallas as pl
from jax.experimental.pallas import tpu as pltpu
from jax.sharding import PartitionSpec as P

FINE_DEGREE = 5
COARSE_DEGREE = 16
OUTER = 2
LOW_FINE = 0.2
LOW_COARSE = 0.02
HIGH_BOUND = 2.0
DAMPING = 0.5
H1 = 6
MESH = pl.DeviceIdType.MESH
F32 = jnp.float32


def cheb_steps(degree, low, high):
    theta = (high + low) / 2.0
    delta = (high - low) / 2.0
    sigma = theta / delta
    rho = 1.0 / sigma
    keeps = []
    pushes = []
    for step in range(degree - 1):
        rho_new = 1.0 / (2.0 * sigma - rho)
        keeps.append(rho_new * rho)
        pushes.append(2.0 * rho_new / delta)
        rho = rho_new
    return (1.0 / theta, keeps, pushes)


def dot(a, b):
    return jnp.dot(a, b, precision=lax.Precision.HIGHEST, preferred_element_type=F32)


def loop(low, high, body, unroll):
    whole = (high - low) // unroll
    if whole > 1:

        def several(i, carry):
            for j in range(unroll):
                body(low + i * unroll + j)
            return carry

        lax.fori_loop(0, whole, several, 0)
    else:
        whole = 0
    for p in range(low + whole * unroll, high):
        body(p)


def pick(rows, columns, rule, value=1.0):
    i = lax.broadcasted_iota(jnp.int32, (rows, columns), 0)
    j = lax.broadcasted_iota(jnp.int32, (rows, columns), 1)
    return jnp.where(rule(i, j), value, 0.0).astype(F32)


def build(a, w, inv, low, high, unroll, diag=None):
    rows, lanes = a.shape[-2:]
    i = lax.broadcasted_iota(jnp.int32, (rows, lanes), 0)
    j = lax.broadcasted_iota(jnp.int32, (rows, lanes), 1)

    def body(p):
        c = a[p]
        near = (
            a[p - 1],
            a[p + 1],
            jnp.where(i == 0, 0.0, pltpu.roll(c, 1, 0)),
            jnp.where(i == rows - 1, 0.0, pltpu.roll(c, rows - 1, 0)),
            jnp.where(j == 0, 0.0, pltpu.roll(c, 1, 1)),
            jnp.where(j == lanes - 1, 0.0, pltpu.roll(c, lanes - 1, 1)),
        )
        faces = [0.5 * (c + n) for n in near]
        total = faces[0] + faces[1] + faces[2] + faces[3] + faces[4] + faces[5]
        good = c > 0.0
        inverse = jnp.where(good, 1.0 / jnp.where(good, total, 1.0), 0.0)
        inv[p] = inverse
        if diag is not None:
            diag[p] = total
        for k in range(6):
            w[k, p] = jnp.where(near[k] > 0.0, faces[k] * inverse, 0.0)

    loop(low, high, body, unroll)


def nearby(w, v, p):
    c = v[p]
    rows, lanes = c.shape
    acc = w[0, p] * v[p - 1] + w[1, p] * v[p + 1]
    acc2 = w[2, p] * pltpu.roll(c, 1, 0) + w[3, p] * pltpu.roll(c, rows - 1, 0)
    acc3 = w[4, p] * pltpu.roll(c, 1, 1) + w[5, p] * pltpu.roll(c, lanes - 1, 1)
    return c, acc + (acc2 + acc3)


def first_update(r, inv, t, d, scale, inv_theta, low, high, unroll):
    def body(p):
        start = r[p] * inv[p] * (1.0 / scale)
        t[p] = start
        d[p] = start * inv_theta

    loop(low, high, body, unroll)


def advance(w, t, d, d_next, keep, push, low, high, unroll, total=None):
    def body(p):
        c, acc = nearby(w, d, p)
        left = t[p] - c + acc
        t[p] = left
        new = keep * c + push * left
        d_next[p] = new
        if total is not None:
            total[p] = total[p] + new

    loop(low, high, body, unroll)


def kernel(
    gx_size, gy_size,
    rhs_ref, coef_ref, sol_ref, res_ref,
    f1, w1, inv1, diag1, t1, d1, u1, last,
    f2, w2, inv2, t2, d2, c2,
    gath, f3, w3, inv3, t3, d3, c3,
    f4, w4, inv4, t4, d4, c4,
    pair_send, pair_recv, s1_send, s1_recv, s2_send, s2_recv, gy_send, gy_recv, gx_send, gx_recv,
    out_send, out_recv,
):
    g = lax.axis_index("grp")
    gy = lax.axis_index("gy")
    nx = 2 * gx_size
    xi = 2 * lax.axis_index("gx") + g
    full_x, by, half_z = rhs_ref.shape
    bx = full_x // 2
    lanes1 = 2 * half_z
    lanes = half_z
    y2, y3, y4 = by // 2, f3.shape[2], f4.shape[2]
    b2 = bx // 2
    n3, n4 = f3.shape[1] - 2, f4.shape[1] - 2

    def where_is(x, y):
        return {"grp": lax.rem(x, 2), "gx": lax.div(x, 2), "gy": y}

    def valid(dx, dy):
        x, y = xi + dx, gy + dy
        return (x >= 0) & (x < nx) & (y >= 0) & (y < gy_size)

    def remote(src, dst, send, recv, x, y):
        return pltpu.make_async_remote_copy(
            src_ref=src, dst_ref=dst, send_sem=send, recv_sem=recv,
            device_id=where_is(x, y), device_id_type=MESH,
        )

    def clear1(p):
        for q in range(3):
            f1[q, p] = jnp.zeros(f1.shape[2:], F32)

    loop(0, f1.shape[1], clear1, 1)

    def clear2(p):
        for q in range(3):
            f2[q, p] = jnp.zeros(f2.shape[2:], F32)

    loop(0, f2.shape[1], clear2, 2)
    for q in (0, 1):
        for p in (0, n3 + 1):
            f3[q, p] = jnp.zeros(f3.shape[2:], F32)
        for p in (0, n4 + 1):
            f4[q, p] = jnp.zeros(f4.shape[2:], F32)
    for k in range(FINE_DEGREE):
        for p in (0, n3 + 1):
            d3[k, p] = jnp.zeros(d3.shape[2:], F32)
    for k in range(2):
        for p in (0, n4 + 1):
            d4[k, p] = jnp.zeros(d4.shape[2:], F32)

    around = [(dx, dy) for dx in range(-2, 3) for dy in range(-1, 2) if (dx, dy) != (0, 0)]
    close = [(dx, dy) for dx, dy in around if abs(dx) < 2]

    barrier = pltpu.get_barrier_semaphore()
    for dx, dy in around:

        @pl.when(valid(dx, dy))
        def _(dx=dx, dy=dy):
            pl.semaphore_signal(barrier, 1, device_id=where_is(xi + dx, gy + dy), device_id_type=MESH)

    for o in range(1, gy_size):
        pl.semaphore_signal(barrier, 1, device_id=where_is(xi, lax.rem(gy + o, gy_size)), device_id_type=MESH)
    for o in range(1, nx):
        pl.semaphore_signal(barrier, 1, device_id=where_is(lax.rem(xi + o, nx), gy), device_id_type=MESH)
    count_x = 1 + sum(jnp.where((xi + dx >= 0) & (xi + dx < nx), 1, 0) for dx in (-2, -1, 1, 2))
    count_y = 1 + sum(jnp.where((gy + dy >= 0) & (gy + dy < gy_size), 1, 0) for dy in (-1, 1))
    pl.semaphore_wait(barrier, count_x * count_y - 1 + gy_size - 1 + nx - 1)

    own_x = pl.ds(H1, bx)
    own_y = pl.ds(8, by)
    mine_z = pl.ds(pl.multiple_of(g * half_z, half_z), half_z)
    their_z = pl.ds(pl.multiple_of((1 - g) * half_z, half_z), half_z)
    mine_x = pl.ds(g * bx, bx)
    their_x = pl.ds((1 - g) * bx, bx)
    partner = xi + 1 - 2 * g
    swaps = [
        remote(ref.at[their_x], f1.at[q, own_x, own_y, mine_z], pair_send.at[q], pair_recv.at[q], partner, gy)
        for q, ref in ((0, coef_ref), (1, rhs_ref))
    ]
    for copy in swaps:
        copy.start()
    for q, ref in ((0, coef_ref), (1, rhs_ref)):
        f1[q, own_x, own_y, mine_z] = ref[mine_x]
    arrivals = [
        remote(ref.at[their_x], f1.at[q, own_x, own_y, their_z], pair_send.at[q], pair_recv.at[q], partner, gy)
        for q, ref in ((0, coef_ref), (1, rhs_ref))
    ]
    for copy in swaps:
        copy.wait_send()
    for copy in arrivals:
        copy.wait_recv()

    half_z_mat = pick(lanes1, lanes, lambda i, j: (i >> 1) == j, 0.125)
    half_y_mat = pick(y2, by, lambda i, j: (j >> 1) == i)
    half_z2 = pick(lanes, lanes, lambda i, j: (i >> 1) == j, 0.125)
    quarter_y = [pick(8, y2, lambda i, j, r=r: i == r * (by // 4) + (j >> 1)) for r in range(bx // 4)]
    half_y3 = pick(y4, y3, lambda i, j: (j >> 1) == i)
    twice_z = pick(lanes, lanes, lambda i, j: (j >> 1) == i)
    twice_z1 = pick(lanes, lanes1, lambda i, j: (j >> 1) == i)
    twice_y3 = pick(y3, y4, lambda i, j: (i >> 1) == j)
    twice_y2 = pick(f2.shape[2], y3, lambda i, j: ((gy * y2 - 8 + i) >> 1) == j)
    twice_y1 = pick(f1.shape[2], f2.shape[2], lambda i, j: (i >> 1) + 4 == j)
    spread = [
        pick(y3, gy_size * 8, lambda i, j, r=r: j == (i >> 2) * 8 + r * (by // 4) + (i & 3)) for r in range(bx // 4)
    ]

    fine = cheb_steps(FINE_DEGREE, LOW_FINE, HIGH_BOUND)
    coarse = cheb_steps(COARSE_DEGREE, LOW_COARSE, HIGH_BOUND)

    for outer in range(OUTER):
        q0, count = ((0, 2), (2, 1))[outer]
        qs = pl.ds(q0, count)
        now = q0 + count - 1

        copies1 = []
        for k, (dx, dy) in enumerate(close):
            src_x, dst_x = {
                0: (own_x, own_x),
                1: (pl.ds(bx, H1), pl.ds(0, H1)),
                -1: (pl.ds(H1, H1), pl.ds(H1 + bx, H1)),
            }[dx]
            src_y, dst_y = {
                0: (own_y, own_y),
                1: (pl.ds(by, 8), pl.ds(0, 8)),
                -1: (pl.ds(8, 8), pl.ds(8 + by, 8)),
            }[dy]
            copies1.append((dx, dy, remote(
                f1.at[qs, src_x, src_y], f1.at[qs, dst_x, dst_y],
                s1_send.at[outer, k], s1_recv.at[outer, k], xi + dx, gy + dy,
            )))
        copies2 = []
        for k, (dx, dy) in enumerate(around):
            copies2.append((dx, dy, remote(
                f2.at[qs, pl.ds(2 * b2, b2), pl.ds(8, y2)],
                f2.at[qs, pl.ds(2 * b2 - b2 * dx, b2), pl.ds(8 - y2 * dy, y2)],
                s2_send.at[outer, k], s2_recv.at[outer, k], xi + dx, gy + dy,
            )))

        def start(copies):
            for dx, dy, copy in copies:
                pl.when(valid(dx, dy))(copy.start)

        def finish(copies):
            for dx, dy, copy in copies:
                pl.when(valid(-dx, -dy))(copy.wait_recv)

        def drain(copies):
            for dx, dy, copy in copies:
                pl.when(valid(dx, dy))(copy.wait_send)

        start(copies1)
        for q in range(q0, q0 + count):
            for p in range(b2):
                both = f1[q, H1 + 2 * p, 8 : 8 + by] + f1[q, H1 + 2 * p + 1, 8 : 8 + by]
                f2[q, 2 * b2 + p, 8 : 8 + y2] = dot(half_y_mat, dot(both, half_z_mat))
        start(copies2)
        for q in range(q0, q0 + count):
            tile = jnp.zeros((8, lanes), F32)
            for r in range(bx // 4):
                both = f2[q, 2 * b2 + 2 * r, 8 : 8 + y2] + f2[q, 2 * b2 + 2 * r + 1, 8 : 8 + y2]
                tile = tile + dot(quarter_y[r], dot(both, half_z2))
            gath[q, xi, gy] = tile

        def along_y(o):
            return remote(
                gath.at[qs, xi, gy], gath.at[qs, xi, gy],
                gy_send.at[outer, o], gy_recv.at[outer, o], xi, lax.rem(gy + o, gy_size),
            )

        def from_y(o):
            y = lax.rem(gy + gy_size - o, gy_size)
            return remote(
                gath.at[qs, xi, y], gath.at[qs, xi, y],
                gy_send.at[outer, o], gy_recv.at[outer, o], xi, lax.rem(gy + o, gy_size),
            )

        def along_x(o):
            return remote(
                gath.at[qs, xi], gath.at[qs, xi],
                gx_send.at[outer, o], gx_recv.at[outer, o], lax.rem(xi + o, nx), gy,
            )

        def from_x(o):
            x = lax.rem(xi + nx - o, nx)
            return remote(
                gath.at[qs, x], gath.at[qs, x],
                gx_send.at[outer, o], gx_recv.at[outer, o], lax.rem(xi + o, nx), gy,
            )

        for o in range(1, gy_size):
            along_y(o).start()
        for o in range(1, gy_size):
            from_y(o).wait_recv()
        for o in range(1, nx):
            along_x(o).start()

        finish(copies2)
        low, high = 2 * b2 - 5, 3 * b2 + 5
        if outer == 0:
            build(f2.at[0], w2, inv2, low, high, 2)
        first_update(f2.at[now], inv2, t2, d2.at[0], 0.25, fine[0], low, high, 7)
        for k in range(FINE_DEGREE - 1):
            low, high = low + 1, high - 1
            advance(w2, t2, d2.at[k], d2.at[k + 1], fine[1][k], fine[2][k], low, high, 4)
        low2 = low

        for o in range(1, nx):
            from_x(o).wait_recv()
        for q in range(q0, q0 + count):
            slot = 0 if q == 0 else 1

            def unpack(x, q=q, slot=slot):
                tiles = gath[q, x].reshape(gy_size * 8, lanes)
                for r in range(bx // 4):
                    f3[slot, 1 + x * (bx // 4) + r] = dot(spread[r], tiles)

            loop(0, nx, unpack, 4)

            def shrink(x, slot=slot):
                both = f3[slot, 1 + 2 * x] + f3[slot, 2 + 2 * x]
                f4[slot, 1 + x] = dot(half_y3, dot(both, half_z2))

            loop(0, n4, shrink, 4)
        if outer == 0:
            build(f3.at[0], w3, inv3, 1, n3 + 1, 4)
            build(f4.at[0], w4, inv4, 1, n4 + 1, 4)
        first_update(f4.at[1], inv4, t4, d4.at[0], 0.015625, coarse[0], 1, n4 + 1, 8)

        def begin4(p):
            c4[p] = d4[0, p]

        loop(1, n4 + 1, begin4, 8)
        for k in range(COARSE_DEGREE - 1):
            advance(w4, t4, d4.at[k % 2], d4.at[(k + 1) % 2], coarse[1][k], coarse[2][k], 1, n4 + 1, 8, c4)
        first_update(f3.at[1], inv3, t3, d3.at[0], 0.0625, fine[0], 1, n3 + 1, 8)
        for k in range(FINE_DEGREE - 1):
            advance(w3, t3, d3.at[k], d3.at[k + 1], fine[1][k], fine[2][k], 1, n3 + 1, 4)

        def combine3(x):
            wide = dot(twice_y3, dot(c4[1 + x], twice_z))
            for p in (1 + 2 * x, 2 + 2 * x):
                c3[p] = ((d3[0, p] + d3[1, p]) + (d3[2, p] + d3[3, p])) + d3[4, p] + wide

        loop(0, n4, combine3, 4)
        b3 = b2 // 2
        for r in range(-1, b3 + 1):
            plane = jnp.clip(xi * b3 + r, 0, n3 - 1) + 1
            wide = dot(twice_y2, dot(c3[plane], twice_z))
            for p in (2 * b2 + 2 * r, 2 * b2 + 2 * r + 1):
                if 2 * b2 - 1 <= p < 3 * b2 + 1:
                    c2[p] = ((d2[0, p] + d2[1, p]) + (d2[2, p] + d2[3, p])) + d2[4, p] + wide

        finish(copies1)
        low, high = H1 - 5, H1 + bx + 5
        if outer == 0:
            build(f1.at[0], w1, inv1, low, high, 1, diag1)
        first_update(f1.at[now], inv1, t1, d1.at[0], 1.0, fine[0], low, high, 2)
        for k in range(FINE_DEGREE - 1):
            low, high = low + 1, high - 1
            advance(w1, t1, d1.at[k], d1.at[k + 1], fine[1][k], fine[2][k], low, high, 2)

        def combine1(r):
            wide = dot(twice_y1, dot(c2[2 * b2 + r], twice_z1))
            return wide

        for r in range(-1, b2 + 1):
            wide = combine1(r)
            for p in (H1 + 2 * r, H1 + 2 * r + 1):
                if H1 - 1 <= p < H1 + bx + 1:
                    both = ((d1[0, p] + d1[1, p]) + (d1[2, p] + d1[3, p])) + d1[4, p] + wide
                    if outer == 0:
                        u1[p] = DAMPING * both
                    else:
                        u1[p] = u1[p] + DAMPING * both

        def leftover(p):
            c, acc = nearby(w1, u1, p)
            value = f1[1, p] - diag1[p] * (c - acc)
            if outer + 1 < OUTER:
                f1[2, p, 8 : 8 + by] = value[8 : 8 + by]
            else:
                last[p - H1] = value[8 : 8 + by]

        loop(H1, H1 + bx, leftover, 2)
        drain(copies1)
        drain(copies2)
        for o in range(1, gy_size):
            along_y(o).wait_send()
        for o in range(1, nx):
            along_x(o).wait_send()

    outs = [
        remote(u1.at[own_x, own_y, their_z], sol_ref.at[mine_x], out_send.at[0], out_recv.at[0], partner, gy),
        remote(last.at[:, :, their_z], res_ref.at[mine_x], out_send.at[1], out_recv.at[1], partner, gy),
    ]
    for copy in outs:
        copy.start()
    sol_ref[mine_x] = u1[own_x, own_y, mine_z]
    res_ref[mine_x] = last[:, :, mine_z]
    for copy in outs:
        copy.wait_send()
    remote(u1.at[own_x, own_y, their_z], sol_ref.at[their_x], out_send.at[0], out_recv.at[0], partner, gy).wait_recv()
    remote(last.at[:, :, their_z], res_ref.at[their_x], out_send.at[1], out_recv.at[1], partner, gy).wait_recv()


def solution(mesh):
    gx_size, gy_size = mesh.shape["gx"], mesh.shape["gy"]

    def on_device(right_side, coefficient):
        full_x, by, half_z = right_side.shape
        bx = full_x // 2
        nx = 2 * gx_size
        lanes = half_z
        p1, r1, l1 = bx + 2 * H1, by + 16, 2 * half_z
        b2, y2 = bx // 2, by // 2
        p2, r2 = 5 * b2, y2 + 16
        p3, r3 = nx * bx // 4 + 2, gy_size * by // 4
        p4, r4 = nx * bx // 8 + 2, gy_size * by // 8
        vm = lambda *shape: pltpu.VMEM(shape, F32)
        sem = lambda *shape: pltpu.SemaphoreType.DMA(shape)
        return pl.pallas_call(
            functools.partial(kernel, gx_size, gy_size),
            out_shape=(jax.ShapeDtypeStruct(right_side.shape, F32),) * 2,
            in_specs=[pl.BlockSpec(memory_space=pltpu.VMEM)] * 2,
            out_specs=(pl.BlockSpec(memory_space=pltpu.VMEM),) * 2,
            scratch_shapes=[
                vm(3, p1, r1, l1), vm(6, p1, r1, l1), vm(p1, r1, l1), vm(p1, r1, l1), vm(p1, r1, l1),
                vm(FINE_DEGREE, p1, r1, l1), vm(p1, r1, l1), vm(bx, by, l1),
                vm(3, p2, r2, lanes), vm(6, p2, r2, lanes), vm(p2, r2, lanes), vm(p2, r2, lanes),
                vm(FINE_DEGREE, p2, r2, lanes), vm(p2, r2, lanes),
                vm(3, nx, gy_size, 8, lanes),
                vm(2, p3, r3, lanes), vm(6, p3, r3, lanes), vm(p3, r3, lanes), vm(p3, r3, lanes),
                vm(FINE_DEGREE, p3, r3, lanes), vm(p3, r3, lanes),
                vm(2, p4, r4, lanes), vm(6, p4, r4, lanes), vm(p4, r4, lanes), vm(p4, r4, lanes),
                vm(2, p4, r4, lanes), vm(p4, r4, lanes),
                sem(2), sem(2), sem(2, 8), sem(2, 8), sem(2, 14), sem(2, 14),
                sem(2, gy_size), sem(2, gy_size), sem(2, nx), sem(2, nx), sem(2), sem(2),
            ],
            compiler_params=pltpu.CompilerParams(
                collective_id=0, has_side_effects=True, vmem_limit_bytes=48 * 1024 * 1024
            ),
        )(right_side, coefficient)

    placed = (P("gx", "gy", "grp"), P("gx", "gy", "grp"))
    return jax.shard_map(on_device, mesh=mesh, in_specs=placed, out_specs=placed, check_vma=False)
```

```python
import functools

import jax
import jax.numpy as jnp
from jax import lax
from jax.experimental import pallas as pl
from jax.experimental.pallas import tpu as pltpu
from jax.sharding import PartitionSpec as P

FINE_DEGREE = 5
COARSE_DEGREE = 16
OUTER = 2
LOW_FINE = 0.2
LOW_COARSE = 0.02
HIGH_BOUND = 2.0
DAMPING = 0.5
H1 = 6
MESH = pl.DeviceIdType.MESH
F32 = jnp.float32


def cheb_steps(degree, low, high):
    theta = (high + low) / 2.0
    delta = (high - low) / 2.0
    sigma = theta / delta
    rho = 1.0 / sigma
    keeps = []
    pushes = []
    for step in range(degree - 1):
        rho_new = 1.0 / (2.0 * sigma - rho)
        keeps.append(rho_new * rho)
        pushes.append(2.0 * rho_new / delta)
        rho = rho_new
    return (1.0 / theta, keeps, pushes)


def dot(a, b):
    return jnp.dot(a, b, precision=lax.Precision.HIGHEST, preferred_element_type=F32)


def loop(low, high, body, unroll):
    whole = (high - low) // unroll
    if whole > 1:

        def several(i, carry):
            for j in range(unroll):
                body(low + i * unroll + j)
            return carry

        lax.fori_loop(0, whole, several, 0)
    else:
        whole = 0
    for p in range(low + whole * unroll, high):
        body(p)


def pick(rows, columns, rule, value=1.0):
    i = lax.broadcasted_iota(jnp.int32, (rows, columns), 0)
    j = lax.broadcasted_iota(jnp.int32, (rows, columns), 1)
    return jnp.where(rule(i, j), value, 0.0).astype(F32)


def build(a, w, inv, low, high, unroll, diag=None):
    rows, lanes = a.shape[-2:]
    i = lax.broadcasted_iota(jnp.int32, (rows, lanes), 0)
    j = lax.broadcasted_iota(jnp.int32, (rows, lanes), 1)

    def body(p):
        c = a[p]
        near = (
            a[p - 1],
            a[p + 1],
            jnp.where(i == 0, 0.0, pltpu.roll(c, 1, 0)),
            jnp.where(i == rows - 1, 0.0, pltpu.roll(c, rows - 1, 0)),
            jnp.where(j == 0, 0.0, pltpu.roll(c, 1, 1)),
            jnp.where(j == lanes - 1, 0.0, pltpu.roll(c, lanes - 1, 1)),
        )
        faces = [0.5 * (c + n) for n in near]
        total = faces[0] + faces[1] + faces[2] + faces[3] + faces[4] + faces[5]
        good = c > 0.0
        inverse = jnp.where(good, 1.0 / jnp.where(good, total, 1.0), 0.0)
        inv[p] = inverse
        if diag is not None:
            diag[p] = total
        for k in range(6):
            w[k, p] = jnp.where(near[k] > 0.0, faces[k] * inverse, 0.0)

    loop(low, high, body, unroll)


def nearby(w, v, p):
    c = v[p]
    rows, lanes = c.shape
    acc = w[0, p] * v[p - 1] + w[1, p] * v[p + 1]
    acc2 = w[2, p] * pltpu.roll(c, 1, 0) + w[3, p] * pltpu.roll(c, rows - 1, 0)
    acc3 = w[4, p] * pltpu.roll(c, 1, 1) + w[5, p] * pltpu.roll(c, lanes - 1, 1)
    return c, acc + (acc2 + acc3)


def first_update(r, inv, t, d, scale, inv_theta, low, high, unroll):
    def body(p):
        start = r[p] * inv[p] * (1.0 / scale)
        t[p] = start
        d[p] = start * inv_theta

    loop(low, high, body, unroll)


def advance(w, t, d, d_next, keep, push, low, high, unroll, total=None):
    def body(p):
        c, acc = nearby(w, d, p)
        left = t[p] - c + acc
        t[p] = left
        new = keep * c + push * left
        d_next[p] = new
        if total is not None:
            total[p] = total[p] + new

    loop(low, high, body, unroll)


def kernel(
    gx_size, gy_size,
    rhs_ref, coef_ref, sol_ref, res_ref,
    f1, w1, inv1, diag1, t1, d1, u1, last,
    f2, w2, inv2, t2, d2, c2,
    gath, f3, w3, inv3, t3, d3, c3,
    f4, w4, inv4, t4, d4, c4,
    tmp, c1, load_sem,
    pair_send, pair_recv, s1_send, s1_recv, s2_send, s2_recv, gy_send, gy_recv, gx_send, gx_recv,
    out_send, out_recv,
):
    g = lax.axis_index("grp")
    gy = lax.axis_index("gy")
    nx = 2 * gx_size
    xi = 2 * lax.axis_index("gx") + g
    full_x, by, half_z = rhs_ref.shape
    bx = full_x // 2
    lanes1 = 2 * half_z
    lanes = half_z
    y2, y3, y4 = by // 2, f3.shape[2], f4.shape[2]
    b2 = bx // 2
    n3, n4 = f3.shape[1] - 2, f4.shape[1] - 2

    def where_is(x, y):
        return {"grp": lax.rem(x, 2), "gx": lax.div(x, 2), "gy": y}

    def valid(dx, dy):
        x, y = xi + dx, gy + dy
        return (x >= 0) & (x < nx) & (y >= 0) & (y < gy_size)

    def remote(src, dst, send, recv, x, y):
        return pltpu.make_async_remote_copy(
            src_ref=src, dst_ref=dst, send_sem=send, recv_sem=recv,
            device_id=where_is(x, y), device_id_type=MESH,
        )

    def clear1(p):
        for q in range(3):
            f1[q, p] = jnp.zeros(f1.shape[2:], F32)

    loop(0, f1.shape[1], clear1, 1)

    def clear2(p):
        for q in range(3):
            f2[q, p] = jnp.zeros(f2.shape[2:], F32)

    loop(0, f2.shape[1], clear2, 2)
    own_x = pl.ds(H1, bx)
    own_y = pl.ds(8, by)
    mine_z = pl.ds(pl.multiple_of(g * half_z, half_z), half_z)
    their_z = pl.ds(pl.multiple_of((1 - g) * half_z, half_z), half_z)
    mine_x = pl.ds(g * bx, bx)
    their_x = pl.ds((1 - g) * bx, bx)
    partner = xi + 1 - 2 * g
    loads = [
        pltpu.make_async_copy(ref.at[mine_x], f1.at[q, own_x, own_y, mine_z], load_sem.at[q])
        for q, ref in ((0, coef_ref), (1, rhs_ref))
    ]
    for copy in loads:
        copy.start()
    for q in (0, 1):
        for p in (0, n3 + 1):
            f3[q, p] = jnp.zeros(f3.shape[2:], F32)
        for p in (0, n4 + 1):
            f4[q, p] = jnp.zeros(f4.shape[2:], F32)
    for k in range(FINE_DEGREE):
        for p in (0, n3 + 1):
            d3[k, p] = jnp.zeros(d3.shape[2:], F32)
    for k in range(2):
        for p in (0, n4 + 1):
            d4[k, p] = jnp.zeros(d4.shape[2:], F32)

    around = [(dx, dy) for dx in range(-2, 3) for dy in range(-1, 2) if (dx, dy) != (0, 0)]
    close = [(dx, dy) for dx, dy in around if abs(dx) < 2]

    barrier = pltpu.get_barrier_semaphore()
    for dx, dy in around:

        @pl.when(valid(dx, dy))
        def _(dx=dx, dy=dy):
            pl.semaphore_signal(barrier, 1, device_id=where_is(xi + dx, gy + dy), device_id_type=MESH)

    for o in range(1, gy_size):
        pl.semaphore_signal(barrier, 1, device_id=where_is(xi, lax.rem(gy + o, gy_size)), device_id_type=MESH)
    for o in range(1, nx):
        pl.semaphore_signal(barrier, 1, device_id=where_is(lax.rem(xi + o, nx), gy), device_id_type=MESH)
    count_x = 1 + sum(jnp.where((xi + dx >= 0) & (xi + dx < nx), 1, 0) for dx in (-2, -1, 1, 2))
    count_y = 1 + sum(jnp.where((gy + dy >= 0) & (gy + dy < gy_size), 1, 0) for dy in (-1, 1))
    pl.semaphore_wait(barrier, count_x * count_y - 1 + gy_size - 1 + nx - 1)

    swaps = [
        remote(ref.at[their_x], f1.at[q, own_x, own_y, mine_z], pair_send.at[q], pair_recv.at[q], partner, gy)
        for q, ref in ((0, coef_ref), (1, rhs_ref))
    ]
    for copy in swaps:
        copy.start()
    arrivals = [
        remote(ref.at[their_x], f1.at[q, own_x, own_y, their_z], pair_send.at[q], pair_recv.at[q], partner, gy)
        for q, ref in ((0, coef_ref), (1, rhs_ref))
    ]
    for copy in swaps:
        copy.wait_send()
    for copy in arrivals:
        copy.wait_recv()
    for copy in loads:
        copy.wait()

    half_z_mat = pick(lanes1, lanes, lambda i, j: (i >> 1) == j, 0.125)
    half_z2 = pick(lanes, lanes, lambda i, j: (i >> 1) == j, 0.125)
    twice_z = pick(lanes, lanes, lambda i, j: (j >> 1) == i)
    twice_z1 = pick(lanes, lanes1, lambda i, j: (j >> 1) == i)
    rows1, rows2 = f1.shape[2], f2.shape[2]
    b3 = b2 // 2

    def blocks(count, rows, columns, rule):
        def whole(i, j):
            found = False
            for r in range(count):
                a, b = i - r * rows, j - r * columns
                found = found | ((a >= 0) & (a < rows) & (b >= 0) & (b < columns) & rule(a, b))
            return found

        return pick(count * rows, count * columns, whole)

    twice_y2 = blocks(b3 + 2, rows2, y3, lambda i, j: ((gy * y2 - 8 + i) >> 1) == j)
    twice_y1 = blocks(b2 + 2, rows1, rows2, lambda i, j: (i >> 1) + 4 == j)
    upper = lax.broadcasted_iota(jnp.int32, (8, lanes), 0) < 4

    def pairs(value):
        n = value.shape[0]
        tmp[0:n] = value
        return tmp[pl.ds(0, n // 2, 2)] + tmp[pl.ds(1, n // 2, 2)]

    fine = cheb_steps(FINE_DEGREE, LOW_FINE, HIGH_BOUND)
    coarse = cheb_steps(COARSE_DEGREE, LOW_COARSE, HIGH_BOUND)

    for outer in range(OUTER):
        q0, count = ((0, 2), (2, 1))[outer]
        qs = pl.ds(q0, count)
        now = q0 + count - 1

        copies1 = []
        for k, (dx, dy) in enumerate(close):
            src_x, dst_x = {
                0: (own_x, own_x),
                1: (pl.ds(bx, H1), pl.ds(0, H1)),
                -1: (pl.ds(H1, H1), pl.ds(H1 + bx, H1)),
            }[dx]
            src_y, dst_y = {
                0: (own_y, own_y),
                1: (pl.ds(by, 8), pl.ds(0, 8)),
                -1: (pl.ds(8, 8), pl.ds(8 + by, 8)),
            }[dy]
            copies1.append((dx, dy, remote(
                f1.at[qs, src_x, src_y], f1.at[qs, dst_x, dst_y],
                s1_send.at[outer, k], s1_recv.at[outer, k], xi + dx, gy + dy,
            )))
        copies2 = []
        for k, (dx, dy) in enumerate(around):
            copies2.append((dx, dy, remote(
                f2.at[qs, pl.ds(2 * b2, b2), pl.ds(8, y2)],
                f2.at[qs, pl.ds(2 * b2 - b2 * dx, b2), pl.ds(8 - y2 * dy, y2)],
                s2_send.at[outer, k], s2_recv.at[outer, k], xi + dx, gy + dy,
            )))

        def start(copies):
            for dx, dy, copy in copies:
                pl.when(valid(dx, dy))(copy.start)

        def finish(copies):
            for dx, dy, copy in copies:
                pl.when(valid(-dx, -dy))(copy.wait_recv)

        def drain(copies):
            for dx, dy, copy in copies:
                pl.when(valid(dx, dy))(copy.wait_send)

        start(copies1)
        parts = [
            f1[q, H1 + 2 * p, 8 : 8 + by] + f1[q, H1 + 2 * p + 1, 8 : 8 + by]
            for q in range(q0, q0 + count) for p in range(b2)
        ]
        halves = pairs(dot(jnp.concatenate(parts, axis=0), half_z_mat))
        parts = [halves[k * y2 : (k + 1) * y2] for k in range(count * b2)]
        for k in range(count * b2):
            f2[q0 + k // b2, 2 * b2 + k % b2, 8 : 8 + y2] = parts[k]
        start(copies2)
        parts = [parts[2 * k] + parts[2 * k + 1] for k in range(count * b3)]
        halves = pairs(dot(jnp.concatenate(parts, axis=0), half_z2))
        for k in range(count):
            gath[q0 + k, xi, gy] = halves[k * 8 : (k + 1) * 8]

        def along_y(o):
            return remote(
                gath.at[qs, xi, gy], gath.at[qs, xi, gy],
                gy_send.at[outer, o], gy_recv.at[outer, o], xi, lax.rem(gy + o, gy_size),
            )

        def from_y(o):
            y = lax.rem(gy + gy_size - o, gy_size)
            return remote(
                gath.at[qs, xi, y], gath.at[qs, xi, y],
                gy_send.at[outer, o], gy_recv.at[outer, o], xi, lax.rem(gy + o, gy_size),
            )

        def along_x(o):
            return remote(
                gath.at[qs, xi], gath.at[qs, xi],
                gx_send.at[outer, o], gx_recv.at[outer, o], lax.rem(xi + o, nx), gy,
            )

        def from_x(o):
            x = lax.rem(xi + nx - o, nx)
            return remote(
                gath.at[qs, x], gath.at[qs, x],
                gx_send.at[outer, o], gx_recv.at[outer, o], lax.rem(xi + o, nx), gy,
            )

        for o in range(1, gy_size):
            along_y(o).start()
        for o in range(1, gy_size):
            from_y(o).wait_recv()
        for o in range(1, nx):
            along_x(o).start()

        finish(copies2)
        low, high = 2 * b2 - 5, 3 * b2 + 5
        if outer == 0:
            build(f2.at[0], w2, inv2, low, high, 2)
        first_update(f2.at[now], inv2, t2, d2.at[0], 0.25, fine[0], low, high, 7)
        for k in range(FINE_DEGREE - 1):
            low, high = low + 1, high - 1
            advance(w2, t2, d2.at[k], d2.at[k + 1], fine[1][k], fine[2][k], low, high, 4)
        low2 = low

        for o in range(1, nx):
            from_x(o).wait_recv()
        for q in range(q0, q0 + count):
            slot = 0 if q == 0 else 1

            def unpack(x, q=q, slot=slot):
                for k in range(gy_size // 2):
                    even, odd = gath[q, x, 2 * k], gath[q, x, 2 * k + 1]
                    place = slice(8 * k, 8 * k + 8)
                    f3[slot, 1 + 2 * x, place] = jnp.where(upper, even, pltpu.roll(odd, 4, 0))
                    f3[slot, 2 + 2 * x, place] = jnp.where(upper, pltpu.roll(even, 4, 0), odd)

            loop(0, nx, unpack, 4)

        slots = (0, 1) if count == 2 else (1,)
        parts = [f3[slot, 1 + 2 * x] + f3[slot, 2 + 2 * x] for slot in slots for x in range(n4)]
        halves = pairs(dot(jnp.concatenate(parts, axis=0), half_z2))
        for k in range(count * n4):
            f4[slots[k // n4], 1 + k % n4] = halves[k * y4 : (k + 1) * y4]
        if outer == 0:
            build(f3.at[0], w3, inv3, 1, n3 + 1, 4)
            build(f4.at[0], w4, inv4, 1, n4 + 1, 4)
        first_update(f4.at[1], inv4, t4, d4.at[0], 0.015625, coarse[0], 1, n4 + 1, 8)

        def begin4(p):
            c4[p] = d4[0, p]

        loop(1, n4 + 1, begin4, 8)
        for k in range(COARSE_DEGREE - 1):
            advance(w4, t4, d4.at[k % 2], d4.at[(k + 1) % 2], coarse[1][k], coarse[2][k], 1, n4 + 1, 8, c4)
        first_update(f3.at[1], inv3, t3, d3.at[0], 0.0625, fine[0], 1, n3 + 1, 8)
        for k in range(FINE_DEGREE - 1):
            advance(w3, t3, d3.at[k], d3.at[k + 1], fine[1][k], fine[2][k], 1, n3 + 1, 4)

        wide = dot(jnp.concatenate([c4[1 + x] for x in range(n4)], axis=0), twice_z)
        tmp[pl.ds(0, n4 * y4, 2)] = wide
        tmp[pl.ds(1, n4 * y4, 2)] = wide
        for x in range(n4):
            add = tmp[x * y3 : (x + 1) * y3]
            for p in (1 + 2 * x, 2 + 2 * x):
                c3[p] = ((d3[0, p] + d3[1, p]) + (d3[2, p] + d3[3, p])) + d3[4, p] + add
        parts = [c3[jnp.clip(xi * b3 + r, 0, n3 - 1) + 1] for r in range(-1, b3 + 1)]
        wide = dot(twice_y2, dot(jnp.concatenate(parts, axis=0), twice_z))
        for r in range(-1, b3 + 1):
            add = wide[(r + 1) * rows2 : (r + 2) * rows2]
            for p in (2 * b2 + 2 * r, 2 * b2 + 2 * r + 1):
                if 2 * b2 - 1 <= p < 3 * b2 + 1:
                    c2[p] = ((d2[0, p] + d2[1, p]) + (d2[2, p] + d2[3, p])) + d2[4, p] + add
        parts = [c2[2 * b2 + r] for r in range(-1, b2 + 1)]
        wide1 = dot(twice_y1, dot(jnp.concatenate(parts, axis=0), twice_z1))
        for r in range(b2 + 2):
            c1[r] = wide1[r * rows1 : (r + 1) * rows1]

        finish(copies1)
        low, high = H1 - 5, H1 + bx + 5
        if outer == 0:
            build(f1.at[0], w1, inv1, low, high, 1, diag1)
        first_update(f1.at[now], inv1, t1, d1.at[0], 1.0, fine[0], low, high, 2)
        for k in range(FINE_DEGREE - 1):
            low, high = low + 1, high - 1
            advance(w1, t1, d1.at[k], d1.at[k + 1], fine[1][k], fine[2][k], low, high, 2)

        for r in range(-1, b2 + 1):
            add = c1[r + 1]
            for p in (H1 + 2 * r, H1 + 2 * r + 1):
                if H1 - 1 <= p < H1 + bx + 1:
                    both = ((d1[0, p] + d1[1, p]) + (d1[2, p] + d1[3, p])) + d1[4, p] + add
                    if outer == 0:
                        u1[p] = DAMPING * both
                    else:
                        u1[p] = u1[p] + DAMPING * both

        def leftover(p):
            c, acc = nearby(w1, u1, p)
            value = f1[1, p] - diag1[p] * (c - acc)
            if outer + 1 < OUTER:
                f1[2, p, 8 : 8 + by] = value[8 : 8 + by]
            else:
                last[p - H1] = value[8 : 8 + by]

        loop(H1, H1 + bx, leftover, 2)
        drain(copies1)
        drain(copies2)
        for o in range(1, gy_size):
            along_y(o).wait_send()
        for o in range(1, nx):
            along_x(o).wait_send()

    outs = [
        remote(u1.at[own_x, own_y, their_z], sol_ref.at[mine_x], out_send.at[0], out_recv.at[0], partner, gy),
        remote(last.at[:, :, their_z], res_ref.at[mine_x], out_send.at[1], out_recv.at[1], partner, gy),
    ]
    for copy in outs:
        copy.start()
    sol_ref[mine_x] = u1[own_x, own_y, mine_z]
    res_ref[mine_x] = last[:, :, mine_z]
    for copy in outs:
        copy.wait_send()
    remote(u1.at[own_x, own_y, their_z], sol_ref.at[their_x], out_send.at[0], out_recv.at[0], partner, gy).wait_recv()
    remote(last.at[:, :, their_z], res_ref.at[their_x], out_send.at[1], out_recv.at[1], partner, gy).wait_recv()


def solution(mesh):
    gx_size, gy_size = mesh.shape["gx"], mesh.shape["gy"]

    def on_device(right_side, coefficient):
        full_x, by, half_z = right_side.shape
        bx = full_x // 2
        nx = 2 * gx_size
        lanes = half_z
        p1, r1, l1 = bx + 2 * H1, by + 16, 2 * half_z
        b2, y2 = bx // 2, by // 2
        p2, r2 = 5 * b2, y2 + 16
        p3, r3 = nx * bx // 4 + 2, gy_size * by // 4
        p4, r4 = nx * bx // 8 + 2, gy_size * by // 8
        vm = lambda *shape: pltpu.VMEM(shape, F32)
        sem = lambda *shape: pltpu.SemaphoreType.DMA(shape)
        return pl.pallas_call(
            functools.partial(kernel, gx_size, gy_size),
            out_shape=(jax.ShapeDtypeStruct(right_side.shape, F32),) * 2,
            in_specs=[pl.BlockSpec(memory_space=pltpu.HBM)] * 2,
            out_specs=(pl.BlockSpec(memory_space=pltpu.VMEM),) * 2,
            scratch_shapes=[
                vm(3, p1, r1, l1), vm(6, p1, r1, l1), vm(p1, r1, l1), vm(p1, r1, l1), vm(p1, r1, l1),
                vm(FINE_DEGREE, p1, r1, l1), vm(p1, r1, l1), vm(bx, by, l1),
                vm(3, p2, r2, lanes), vm(6, p2, r2, lanes), vm(p2, r2, lanes), vm(p2, r2, lanes),
                vm(FINE_DEGREE, p2, r2, lanes), vm(p2, r2, lanes),
                vm(3, nx, gy_size, 8, lanes),
                vm(2, p3, r3, lanes), vm(6, p3, r3, lanes), vm(p3, r3, lanes), vm(p3, r3, lanes),
                vm(FINE_DEGREE, p3, r3, lanes), vm(p3, r3, lanes),
                vm(2, p4, r4, lanes), vm(6, p4, r4, lanes), vm(p4, r4, lanes), vm(p4, r4, lanes),
                vm(2, p4, r4, lanes), vm(p4, r4, lanes),
                vm(max((p3 - 2) * r3, 2 * b2 * by), lanes), vm(b2 + 2, r1, l1), sem(2),
                sem(2), sem(2), sem(2, 8), sem(2, 8), sem(2, 14), sem(2, 14),
                sem(2, gy_size), sem(2, gy_size), sem(2, nx), sem(2, nx), sem(2), sem(2),
            ],
            compiler_params=pltpu.CompilerParams(
                collective_id=0, has_side_effects=True, vmem_limit_bytes=64 * 1024 * 1024
            ),
        )(right_side, coefficient)

    placed = (P("gx", "gy", "grp"), P("gx", "gy", "grp"))
    return jax.shard_map(on_device, mesh=mesh, in_specs=placed, out_specs=placed, check_vma=False)
```

```python
import functools

import jax
import jax.numpy as jnp
from jax import lax
from jax.experimental import pallas as pl
from jax.experimental.pallas import tpu as pltpu
from jax.sharding import PartitionSpec as P

FINE_DEGREE = 5
COARSE_DEGREE = 16
OUTER = 2
LOW_FINE = 0.2
LOW_COARSE = 0.02
HIGH_BOUND = 2.0
DAMPING = 0.5
H1 = 6
MESH = pl.DeviceIdType.MESH
F32 = jnp.float32


def cheb_steps(degree, low, high):
    theta = (high + low) / 2.0
    delta = (high - low) / 2.0
    sigma = theta / delta
    rho = 1.0 / sigma
    keeps = []
    pushes = []
    for step in range(degree - 1):
        rho_new = 1.0 / (2.0 * sigma - rho)
        keeps.append(rho_new * rho)
        pushes.append(2.0 * rho_new / delta)
        rho = rho_new
    return (1.0 / theta, keeps, pushes)


def dot(a, b):
    return jnp.dot(a, b, precision=lax.Precision.HIGHEST, preferred_element_type=F32)


def loop(low, high, body, unroll):
    whole = (high - low) // unroll
    if whole > 1:

        def several(i, carry):
            for j in range(unroll):
                body(low + i * unroll + j)
            return carry

        lax.fori_loop(0, whole, several, 0)
    else:
        whole = 0
    for p in range(low + whole * unroll, high):
        body(p)


def pick(rows, columns, rule, value=1.0):
    i = lax.broadcasted_iota(jnp.int32, (rows, columns), 0)
    j = lax.broadcasted_iota(jnp.int32, (rows, columns), 1)
    return jnp.where(rule(i, j), value, 0.0).astype(F32)


def build(a, w, inv, low, high, unroll, diag=None):
    rows, lanes = a.shape[-2:]
    i = lax.broadcasted_iota(jnp.int32, (rows, lanes), 0)
    j = lax.broadcasted_iota(jnp.int32, (rows, lanes), 1)

    def body(p):
        c = a[p]
        near = (
            a[p - 1],
            a[p + 1],
            jnp.where(i == 0, 0.0, pltpu.roll(c, 1, 0)),
            jnp.where(i == rows - 1, 0.0, pltpu.roll(c, rows - 1, 0)),
            jnp.where(j == 0, 0.0, pltpu.roll(c, 1, 1)),
            jnp.where(j == lanes - 1, 0.0, pltpu.roll(c, lanes - 1, 1)),
        )
        faces = [0.5 * (c + n) for n in near]
        total = faces[0] + faces[1] + faces[2] + faces[3] + faces[4] + faces[5]
        good = c > 0.0
        inverse = jnp.where(good, 1.0 / jnp.where(good, total, 1.0), 0.0)
        inv[p] = inverse
        if diag is not None:
            diag[p] = total
        for k in range(6):
            w[k, p] = jnp.where(near[k] > 0.0, faces[k] * inverse, 0.0)

    loop(low, high, body, unroll)


def nearby(w, v, p):
    c = v[p]
    rows, lanes = c.shape
    acc = w[0, p] * v[p - 1] + w[1, p] * v[p + 1]
    acc2 = w[2, p] * pltpu.roll(c, 1, 0) + w[3, p] * pltpu.roll(c, rows - 1, 0)
    acc3 = w[4, p] * pltpu.roll(c, 1, 1) + w[5, p] * pltpu.roll(c, lanes - 1, 1)
    return c, acc + (acc2 + acc3)


def first_update(r, inv, t, d, scale, inv_theta, low, high, unroll):
    def body(p):
        start = r[p] * inv[p] * (1.0 / scale)
        t[p] = start
        d[p] = start * inv_theta

    loop(low, high, body, unroll)


def advance(w, t, d, d_next, keep, push, low, high, unroll, total=None):
    def body(p):
        c, acc = nearby(w, d, p)
        left = t[p] - c + acc
        t[p] = left
        new = keep * c + push * left
        d_next[p] = new
        if total is not None:
            total[p] = total[p] + new

    loop(low, high, body, unroll)


def kernel(
    gx_size, gy_size,
    rhs_ref, coef_ref, sol_ref, res_ref,
    f1, w1, inv1, diag1, t1, d1, u1, last,
    f2, w2, inv2, t2, d2, c2,
    gath, f3, w3, inv3, t3, d3, c3,
    f4, w4, inv4, t4, d4, c4,
    tmp, c1, load_sem,
    pair_send, pair_recv, s1_send, s1_recv, s2_send, s2_recv, gy_send, gy_recv, gx_send, gx_recv,
    out_send, out_recv,
):
    g = lax.axis_index("grp")
    gy = lax.axis_index("gy")
    nx = 2 * gx_size
    xi = 2 * lax.axis_index("gx") + g
    full_x, by, half_z = rhs_ref.shape
    bx = full_x // 2
    lanes1 = 2 * half_z
    lanes = half_z
    y2, y3, y4 = by // 2, f3.shape[2], f4.shape[2]
    b2 = bx // 2
    n3, n4 = f3.shape[1] - 2, f4.shape[1] - 2

    def where_is(x, y):
        return {"grp": lax.rem(x, 2), "gx": lax.div(x, 2), "gy": y}

    def valid(dx, dy):
        x, y = xi + dx, gy + dy
        return (x >= 0) & (x < nx) & (y >= 0) & (y < gy_size)

    def remote(src, dst, send, recv, x, y):
        return pltpu.make_async_remote_copy(
            src_ref=src, dst_ref=dst, send_sem=send, recv_sem=recv,
            device_id=where_is(x, y), device_id_type=MESH,
        )

    def clear1(p):
        for q in range(3):
            f1[q, p] = jnp.zeros(f1.shape[2:], F32)

    loop(0, f1.shape[1], clear1, 1)

    def clear2(p):
        for q in range(3):
            f2[q, p] = jnp.zeros(f2.shape[2:], F32)

    loop(0, f2.shape[1], clear2, 2)
    own_x = pl.ds(H1, bx)
    own_y = pl.ds(8, by)
    mine_z = pl.ds(pl.multiple_of(g * half_z, half_z), half_z)
    their_z = pl.ds(pl.multiple_of((1 - g) * half_z, half_z), half_z)
    mine_x = pl.ds(g * bx, bx)
    their_x = pl.ds((1 - g) * bx, bx)
    partner = xi + 1 - 2 * g
    loads = [
        pltpu.make_async_copy(ref.at[mine_x], f1.at[q, own_x, own_y, mine_z], load_sem.at[q])
        for q, ref in ((0, coef_ref), (1, rhs_ref))
    ]
    for copy in loads:
        copy.start()
    for q in (0, 1):
        for p in (0, n3 + 1):
            f3[q, p] = jnp.zeros(f3.shape[2:], F32)
        for p in (0, n4 + 1):
            f4[q, p] = jnp.zeros(f4.shape[2:], F32)
    for k in range(FINE_DEGREE):
        for p in (0, n3 + 1):
            d3[k, p] = jnp.zeros(d3.shape[2:], F32)
    for k in range(2):
        for p in (0, n4 + 1):
            d4[k, p] = jnp.zeros(d4.shape[2:], F32)

    around = [(dx, dy) for dx in range(-2, 3) for dy in range(-1, 2) if (dx, dy) != (0, 0)]
    close = [(dx, dy) for dx, dy in around if abs(dx) < 2]

    barrier = pltpu.get_barrier_semaphore()
    for dx, dy in around:

        @pl.when(valid(dx, dy))
        def _(dx=dx, dy=dy):
            pl.semaphore_signal(barrier, 1, device_id=where_is(xi + dx, gy + dy), device_id_type=MESH)

    for o in range(1, gy_size):
        pl.semaphore_signal(barrier, 1, device_id=where_is(xi, lax.rem(gy + o, gy_size)), device_id_type=MESH)
    for o in range(1, nx):
        pl.semaphore_signal(barrier, 1, device_id=where_is(lax.rem(xi + o, nx), gy), device_id_type=MESH)
    count_x = 1 + sum(jnp.where((xi + dx >= 0) & (xi + dx < nx), 1, 0) for dx in (-2, -1, 1, 2))
    count_y = 1 + sum(jnp.where((gy + dy >= 0) & (gy + dy < gy_size), 1, 0) for dy in (-1, 1))
    pl.semaphore_wait(barrier, count_x * count_y - 1 + gy_size - 1 + nx - 1)

    swaps = [
        remote(ref.at[their_x], f1.at[q, own_x, own_y, mine_z], pair_send.at[q], pair_recv.at[q], partner, gy)
        for q, ref in ((0, coef_ref), (1, rhs_ref))
    ]
    for copy in swaps:
        copy.start()
    arrivals = [
        remote(ref.at[their_x], f1.at[q, own_x, own_y, their_z], pair_send.at[q], pair_recv.at[q], partner, gy)
        for q, ref in ((0, coef_ref), (1, rhs_ref))
    ]
    for copy in swaps:
        copy.wait_send()
    for copy in arrivals:
        copy.wait_recv()
    for copy in loads:
        copy.wait()

    half_z_mat = pick(lanes1, lanes, lambda i, j: (i >> 1) == j, 0.125)
    half_z2 = pick(lanes, lanes, lambda i, j: (i >> 1) == j, 0.125)
    twice_z = pick(lanes, lanes, lambda i, j: (j >> 1) == i)
    twice_z1 = pick(lanes, lanes1, lambda i, j: (j >> 1) == i)
    rows1, rows2 = f1.shape[2], f2.shape[2]
    b3 = b2 // 2

    def blocks(count, rows, columns, rule):
        def whole(i, j):
            found = False
            for r in range(count):
                a, b = i - r * rows, j - r * columns
                found = found | ((a >= 0) & (a < rows) & (b >= 0) & (b < columns) & rule(a, b))
            return found

        return pick(count * rows, count * columns, whole)

    twice_y2 = blocks(b3 + 2, rows2, y3, lambda i, j: ((gy * y2 - 8 + i) >> 1) == j)
    twice_y1 = blocks(b2 + 2, rows1, rows2, lambda i, j: (i >> 1) + 4 == j)
    upper = lax.broadcasted_iota(jnp.int32, (8, lanes), 0) < 4

    def pairs(value):
        n = value.shape[0]
        tmp[0:n] = value
        return tmp[pl.ds(0, n // 2, 2)] + tmp[pl.ds(1, n // 2, 2)]

    fine = cheb_steps(FINE_DEGREE, LOW_FINE, HIGH_BOUND)
    coarse = cheb_steps(COARSE_DEGREE, LOW_COARSE, HIGH_BOUND)

    for outer in range(OUTER):
        q0, count = ((0, 2), (2, 1))[outer]
        qs = pl.ds(q0, count)
        now = q0 + count - 1

        copies1 = []
        for k, (dx, dy) in enumerate(close):
            h = H1 - outer - (1 if dy else 0)
            src_x, dst_x = {
                0: (own_x, own_x),
                1: (pl.ds(H1 + bx - h, h), pl.ds(H1 - h, h)),
                -1: (pl.ds(H1, h), pl.ds(H1 + bx, h)),
            }[dx]
            src_y, dst_y = {
                0: (own_y, own_y),
                1: (pl.ds(by, 8), pl.ds(0, 8)),
                -1: (pl.ds(8, 8), pl.ds(8 + by, 8)),
            }[dy]
            copies1.append((dx, dy, remote(
                f1.at[qs, src_x, src_y], f1.at[qs, dst_x, dst_y],
                s1_send.at[outer, k], s1_recv.at[outer, k], xi + dx, gy + dy,
            )))
        copies2 = []
        for k, (dx, dy) in enumerate(around):
            if outer and abs(dx) == 2 and dy:
                continue
            copies2.append((dx, dy, remote(
                f2.at[qs, pl.ds(2 * b2, b2), pl.ds(8, y2)],
                f2.at[qs, pl.ds(2 * b2 - b2 * dx, b2), pl.ds(8 - y2 * dy, y2)],
                s2_send.at[outer, k], s2_recv.at[outer, k], xi + dx, gy + dy,
            )))

        def start(copies):
            for dx, dy, copy in copies:
                pl.when(valid(dx, dy))(copy.start)

        def finish(copies):
            for dx, dy, copy in copies:
                pl.when(valid(-dx, -dy))(copy.wait_recv)

        def drain(copies):
            for dx, dy, copy in copies:
                pl.when(valid(dx, dy))(copy.wait_send)

        parts = [
            f1[q, H1 + 2 * p, 8 : 8 + by] + f1[q, H1 + 2 * p + 1, 8 : 8 + by]
            for q in range(q0, q0 + count) for p in range(b2)
        ]
        halves = pairs(dot(jnp.concatenate(parts, axis=0), half_z_mat))
        parts = [halves[k * y2 : (k + 1) * y2] for k in range(count * b2)]
        for k in range(count * b2):
            f2[q0 + k // b2, 2 * b2 + k % b2, 8 : 8 + y2] = parts[k]
        start(copies2)
        parts = [parts[2 * k] + parts[2 * k + 1] for k in range(count * b3)]
        halves = pairs(dot(jnp.concatenate(parts, axis=0), half_z2))
        for k in range(count):
            gath[q0 + k, xi, gy] = halves[k * 8 : (k + 1) * 8]

        def along_y(o):
            return remote(
                gath.at[qs, xi, gy], gath.at[qs, xi, gy],
                gy_send.at[outer, o], gy_recv.at[outer, o], xi, lax.rem(gy + o, gy_size),
            )

        def from_y(o):
            y = lax.rem(gy + gy_size - o, gy_size)
            return remote(
                gath.at[qs, xi, y], gath.at[qs, xi, y],
                gy_send.at[outer, o], gy_recv.at[outer, o], xi, lax.rem(gy + o, gy_size),
            )

        def along_x(o):
            return remote(
                gath.at[qs, xi], gath.at[qs, xi],
                gx_send.at[outer, o], gx_recv.at[outer, o], lax.rem(xi + o, nx), gy,
            )

        def from_x(o):
            x = lax.rem(xi + nx - o, nx)
            return remote(
                gath.at[qs, x], gath.at[qs, x],
                gx_send.at[outer, o], gx_recv.at[outer, o], lax.rem(xi + o, nx), gy,
            )

        for o in range(1, gy_size):
            along_y(o).start()
        for o in range(1, gy_size):
            from_y(o).wait_recv()
        for o in range(1, nx):
            along_x(o).start()

        start(copies1)
        finish(copies2)

        for o in range(1, nx):
            from_x(o).wait_recv()
        for q in range(q0, q0 + count):
            slot = 0 if q == 0 else 1

            def unpack(x, q=q, slot=slot):
                for k in range(gy_size // 2):
                    even, odd = gath[q, x, 2 * k], gath[q, x, 2 * k + 1]
                    place = slice(8 * k, 8 * k + 8)
                    f3[slot, 1 + 2 * x, place] = jnp.where(upper, even, pltpu.roll(odd, 4, 0))
                    f3[slot, 2 + 2 * x, place] = jnp.where(upper, pltpu.roll(even, 4, 0), odd)

            loop(0, nx, unpack, 4)

        slots = (0, 1) if count == 2 else (1,)
        parts = [f3[slot, 1 + 2 * x] + f3[slot, 2 + 2 * x] for slot in slots for x in range(n4)]
        halves = pairs(dot(jnp.concatenate(parts, axis=0), half_z2))
        for k in range(count * n4):
            f4[slots[k // n4], 1 + k % n4] = halves[k * y4 : (k + 1) * y4]
        low, high = 2 * b2 - 5, 3 * b2 + 5
        if outer == 0:
            build(f4.at[0], w4, inv4, 1, n4 + 1, 8)
            build(f3.at[0], w3, inv3, 1, n3 + 1, 4)
            build(f2.at[0], w2, inv2, low, high, 4)
        small = n4 * y4 <= 64
        width = 16 if small else 4
        first_update(f4.at[1], inv4, t4, d4.at[0], 0.015625, coarse[0], 1, n4 + 1, 8)
        first_update(f3.at[1], inv3, t3, d3.at[0], 0.0625, fine[0], 1, n3 + 1, width)
        first_update(f2.at[now], inv2, t2, d2.at[0], 0.25, fine[0], low, high, 16)
        if small:
            zero = jnp.zeros((y4, lanes), F32)
            vs = [d4[0, 1 + p] for p in range(n4)]
            ts = [t4[1 + p] for p in range(n4)]
            sums = list(vs)
        else:

            def begin4(p):
                c4[p] = d4[0, p]

            loop(1, n4 + 1, begin4, 8)
        for k in range(COARSE_DEGREE - 1):
            if small:
                edged = [zero] + vs + [zero]
                news = []
                for p in range(n4):
                    c = vs[p]
                    acc = w4[0, 1 + p] * edged[p] + w4[1, 1 + p] * edged[p + 2]
                    acc2 = w4[2, 1 + p] * pltpu.roll(c, 1, 0) + w4[3, 1 + p] * pltpu.roll(c, y4 - 1, 0)
                    acc3 = w4[4, 1 + p] * pltpu.roll(c, 1, 1) + w4[5, 1 + p] * pltpu.roll(c, lanes - 1, 1)
                    ts[p] = ts[p] - c + (acc + (acc2 + acc3))
                    news.append(coarse[1][k] * c + coarse[2][k] * ts[p])
                    sums[p] = sums[p] + news[p]
                vs = news
            else:
                advance(w4, t4, d4.at[k % 2], d4.at[(k + 1) % 2], coarse[1][k], coarse[2][k], 1, n4 + 1, 8, c4)
            if k % 3 == 0 and k // 3 < FINE_DEGREE - 1:
                m = k // 3
                advance(w3, t3, d3.at[m], d3.at[m + 1], fine[1][m], fine[2][m], 1, n3 + 1, width)
                low, high = low + 1, high - 1
                advance(w2, t2, d2.at[m], d2.at[m + 1], fine[1][m], fine[2][m], low, high, 16)
        if small:
            for p in range(n4):
                c4[1 + p] = sums[p]

        wide = dot(jnp.concatenate([c4[1 + x] for x in range(n4)], axis=0), twice_z)
        tmp[pl.ds(0, n4 * y4, 2)] = wide
        tmp[pl.ds(1, n4 * y4, 2)] = wide
        for x in range(n4):
            add = tmp[x * y3 : (x + 1) * y3]
            for p in (1 + 2 * x, 2 + 2 * x):
                c3[p] = ((d3[0, p] + d3[1, p]) + (d3[2, p] + d3[3, p])) + d3[4, p] + add
        parts = [c3[jnp.clip(xi * b3 + r, 0, n3 - 1) + 1] for r in range(-1, b3 + 1)]
        wide = dot(twice_y2, dot(jnp.concatenate(parts, axis=0), twice_z))
        for r in range(-1, b3 + 1):
            add = wide[(r + 1) * rows2 : (r + 2) * rows2]
            for p in (2 * b2 + 2 * r, 2 * b2 + 2 * r + 1):
                if 2 * b2 - 1 <= p < 3 * b2 + 1:
                    c2[p] = ((d2[0, p] + d2[1, p]) + (d2[2, p] + d2[3, p])) + d2[4, p] + add
        parts = [c2[2 * b2 + r] for r in range(-1, b2 + 1)]
        wide1 = dot(twice_y1, dot(jnp.concatenate(parts, axis=0), twice_z1))
        for r in range(b2 + 2):
            c1[r] = wide1[r * rows1 : (r + 1) * rows1]

        finish(copies1)
        low, high = H1 - 5, H1 + bx + 5
        if outer == 0:
            build(f1.at[0], w1, inv1, low, high, 1, diag1)
        first_update(f1.at[now], inv1, t1, d1.at[0], 1.0, fine[0], low, high, 2)
        for k in range(FINE_DEGREE - 1):
            low, high = low + 1, high - 1
            advance(w1, t1, d1.at[k], d1.at[k + 1], fine[1][k], fine[2][k], low, high, 4)

        for r in range(-1, b2 + 1):
            add = c1[r + 1]
            for p in (H1 + 2 * r, H1 + 2 * r + 1):
                if H1 - 1 <= p < H1 + bx + 1:
                    both = ((d1[0, p] + d1[1, p]) + (d1[2, p] + d1[3, p])) + d1[4, p] + add
                    if outer == 0:
                        u1[p] = DAMPING * both
                    else:
                        u1[p] = u1[p] + DAMPING * both

        def leftover(p):
            c, acc = nearby(w1, u1, p)
            value = f1[1, p] - diag1[p] * (c - acc)
            if outer + 1 < OUTER:
                f1[2, p, 8 : 8 + by] = value[8 : 8 + by]
            else:
                last[p - H1] = value[8 : 8 + by]

        loop(H1, H1 + bx, leftover, 2)
        drain(copies1)
        drain(copies2)
        for o in range(1, gy_size):
            along_y(o).wait_send()
        for o in range(1, nx):
            along_x(o).wait_send()

    outs = [
        remote(u1.at[own_x, own_y, their_z], sol_ref.at[mine_x], out_send.at[0], out_recv.at[0], partner, gy),
        remote(last.at[:, :, their_z], res_ref.at[mine_x], out_send.at[1], out_recv.at[1], partner, gy),
    ]
    for copy in outs:
        copy.start()
    sol_ref[mine_x] = u1[own_x, own_y, mine_z]
    res_ref[mine_x] = last[:, :, mine_z]
    for copy in outs:
        copy.wait_send()
    remote(u1.at[own_x, own_y, their_z], sol_ref.at[their_x], out_send.at[0], out_recv.at[0], partner, gy).wait_recv()
    remote(last.at[:, :, their_z], res_ref.at[their_x], out_send.at[1], out_recv.at[1], partner, gy).wait_recv()


def solution(mesh):
    gx_size, gy_size = mesh.shape["gx"], mesh.shape["gy"]

    def on_device(right_side, coefficient):
        full_x, by, half_z = right_side.shape
        bx = full_x // 2
        nx = 2 * gx_size
        lanes = half_z
        p1, r1, l1 = bx + 2 * H1, by + 16, 2 * half_z
        b2, y2 = bx // 2, by // 2
        p2, r2 = 5 * b2, y2 + 16
        p3, r3 = nx * bx // 4 + 2, gy_size * by // 4
        p4, r4 = nx * bx // 8 + 2, gy_size * by // 8
        vm = lambda *shape: pltpu.VMEM(shape, F32)
        sem = lambda *shape: pltpu.SemaphoreType.DMA(shape)
        return pl.pallas_call(
            functools.partial(kernel, gx_size, gy_size),
            out_shape=(jax.ShapeDtypeStruct(right_side.shape, F32),) * 2,
            in_specs=[pl.BlockSpec(memory_space=pltpu.HBM)] * 2,
            out_specs=(pl.BlockSpec(memory_space=pltpu.VMEM),) * 2,
            scratch_shapes=[
                vm(3, p1, r1, l1), vm(6, p1, r1, l1), vm(p1, r1, l1), vm(p1, r1, l1), vm(p1, r1, l1),
                vm(FINE_DEGREE, p1, r1, l1), vm(p1, r1, l1), vm(bx, by, l1),
                vm(3, p2, r2, lanes), vm(6, p2, r2, lanes), vm(p2, r2, lanes), vm(p2, r2, lanes),
                vm(FINE_DEGREE, p2, r2, lanes), vm(p2, r2, lanes),
                vm(3, nx, gy_size, 8, lanes),
                vm(2, p3, r3, lanes), vm(6, p3, r3, lanes), vm(p3, r3, lanes), vm(p3, r3, lanes),
                vm(FINE_DEGREE, p3, r3, lanes), vm(p3, r3, lanes),
                vm(2, p4, r4, lanes), vm(6, p4, r4, lanes), vm(p4, r4, lanes), vm(p4, r4, lanes),
                vm(2, p4, r4, lanes), vm(p4, r4, lanes),
                vm(max((p3 - 2) * r3, 2 * b2 * by), lanes), vm(b2 + 2, r1, l1), sem(2),
                sem(2), sem(2), sem(2, 8), sem(2, 8), sem(2, 14), sem(2, 14),
                sem(2, gy_size), sem(2, gy_size), sem(2, nx), sem(2, nx), sem(2), sem(2),
            ],
            compiler_params=pltpu.CompilerParams(
                collective_id=0, has_side_effects=True, vmem_limit_bytes=64 * 1024 * 1024
            ),
        )(right_side, coefficient)

    placed = (P("gx", "gy", "grp"), P("gx", "gy", "grp"))
    return jax.shard_map(on_device, mesh=mesh, in_specs=placed, out_specs=placed, check_vma=False)
```

```python
import functools

import jax
import jax.numpy as jnp
from jax import lax
from jax.experimental import pallas as pl
from jax.experimental.pallas import tpu as pltpu
from jax.sharding import PartitionSpec as P

FINE_DEGREE = 5
COARSE_DEGREE = 16
OUTER = 2
LOW_FINE = 0.2
LOW_COARSE = 0.02
HIGH_BOUND = 2.0
DAMPING = 0.5
H1 = 6
MESH = pl.DeviceIdType.MESH
F32 = jnp.float32


def cheb_steps(degree, low, high):
    theta = (high + low) / 2.0
    delta = (high - low) / 2.0
    sigma = theta / delta
    rho = 1.0 / sigma
    keeps = []
    pushes = []
    for step in range(degree - 1):
        rho_new = 1.0 / (2.0 * sigma - rho)
        keeps.append(rho_new * rho)
        pushes.append(2.0 * rho_new / delta)
        rho = rho_new
    return (1.0 / theta, keeps, pushes)


def dot(a, b):
    def times(x, y):
        return jnp.dot(x, y, preferred_element_type=F32)

    if a.dtype == jnp.bfloat16:
        top, middle, rest = thirds(b)
        return times(a, top) + (times(a, middle) + times(a, rest))
    top, middle, rest = thirds(a)
    return times(top, b) + (times(middle, b) + times(rest, b))


def thirds(x):
    top = x.astype(jnp.bfloat16)
    left = x - top.astype(F32)
    middle = left.astype(jnp.bfloat16)
    return top, middle, (left - middle.astype(F32)).astype(jnp.bfloat16)


def loop(low, high, body, unroll):
    whole = (high - low) // unroll
    if whole > 1:

        def several(i, carry):
            for j in range(unroll):
                body(low + i * unroll + j)
            return carry

        lax.fori_loop(0, whole, several, 0)
    else:
        whole = 0
    for p in range(low + whole * unroll, high):
        body(p)


def pick(rows, columns, rule, value=1.0):
    i = lax.broadcasted_iota(jnp.int32, (rows, columns), 0)
    j = lax.broadcasted_iota(jnp.int32, (rows, columns), 1)
    return jnp.where(rule(i, j), value, 0.0).astype(jnp.bfloat16)


def build(a, w, inv, low, high, unroll, diag=None):
    rows, lanes = a.shape[-2:]
    i = lax.broadcasted_iota(jnp.int32, (rows, lanes), 0)
    j = lax.broadcasted_iota(jnp.int32, (rows, lanes), 1)

    def body(p):
        c = a[p]
        near = (
            a[p - 1],
            a[p + 1],
            jnp.where(i == 0, 0.0, pltpu.roll(c, 1, 0)),
            jnp.where(i == rows - 1, 0.0, pltpu.roll(c, rows - 1, 0)),
            jnp.where(j == 0, 0.0, pltpu.roll(c, 1, 1)),
            jnp.where(j == lanes - 1, 0.0, pltpu.roll(c, lanes - 1, 1)),
        )
        faces = [0.5 * (c + n) for n in near]
        total = faces[0] + faces[1] + faces[2] + faces[3] + faces[4] + faces[5]
        good = c > 0.0
        inverse = jnp.where(good, 1.0 / jnp.where(good, total, 1.0), 0.0)
        inv[p] = inverse
        if diag is not None:
            diag[p] = total
        for k in range(6):
            w[k, p] = jnp.where(near[k] > 0.0, faces[k] * inverse, 0.0)

    loop(low, high, body, unroll)


def nearby(w, v, p):
    c = v[p]
    rows, lanes = c.shape
    acc = w[0, p] * v[p - 1] + w[1, p] * v[p + 1]
    acc2 = w[2, p] * pltpu.roll(c, 1, 0) + w[3, p] * pltpu.roll(c, rows - 1, 0)
    acc3 = w[4, p] * pltpu.roll(c, 1, 1) + w[5, p] * pltpu.roll(c, lanes - 1, 1)
    return c, acc + (acc2 + acc3)


def first_update(r, inv, t, d, scale, inv_theta, low, high, unroll):
    def body(p):
        start = r[p] * inv[p] * (1.0 / scale)
        t[p] = start
        d[p] = start * inv_theta

    loop(low, high, body, unroll)


def advance(w, t, d, d_next, keep, push, low, high, unroll, total=None):
    def body(p):
        c, acc = nearby(w, d, p)
        left = t[p] - c + acc
        t[p] = left
        new = keep * c + push * left
        d_next[p] = new
        if total is not None:
            total[p] = total[p] + new

    loop(low, high, body, unroll)


def kernel(
    gx_size, gy_size,
    rhs_ref, coef_ref, sol_ref, res_ref,
    f1, w1, inv1, diag1, t1, d1, u1, last,
    f2, w2, inv2, t2, d2, c2,
    gath, f3, w3, inv3, t3, d3, c3,
    f4, w4, inv4, t4, d4, c4,
    tmp, c1, load_sem,
    pair_send, pair_recv, s1_send, s1_recv, s2_send, s2_recv, gy_send, gy_recv, gx_send, gx_recv,
    out_send, out_recv,
):
    g = lax.axis_index("grp")
    gy = lax.axis_index("gy")
    nx = 2 * gx_size
    xi = 2 * lax.axis_index("gx") + g
    full_x, by, half_z = rhs_ref.shape
    bx = full_x // 2
    lanes1 = 2 * half_z
    lanes = half_z
    y2, y3, y4 = by // 2, f3.shape[2], f4.shape[2]
    b2 = bx // 2
    n3, n4 = f3.shape[1] - 2, f4.shape[1] - 2

    def where_is(x, y):
        return {"grp": lax.rem(x, 2), "gx": lax.div(x, 2), "gy": y}

    def valid(dx, dy):
        x, y = xi + dx, gy + dy
        return (x >= 0) & (x < nx) & (y >= 0) & (y < gy_size)

    def remote(src, dst, send, recv, x, y):
        return pltpu.make_async_remote_copy(
            src_ref=src, dst_ref=dst, send_sem=send, recv_sem=recv,
            device_id=where_is(x, y), device_id_type=MESH,
        )

    def clear1(p):
        for q in range(3):
            f1[q, p] = jnp.zeros(f1.shape[2:], F32)

    loop(0, f1.shape[1], clear1, 1)

    def clear2(p):
        for q in range(3):
            f2[q, p] = jnp.zeros(f2.shape[2:], F32)

    loop(0, f2.shape[1], clear2, 2)
    own_x = pl.ds(H1, bx)
    own_y = pl.ds(8, by)
    mine_z = pl.ds(pl.multiple_of(g * half_z, half_z), half_z)
    their_z = pl.ds(pl.multiple_of((1 - g) * half_z, half_z), half_z)
    mine_x = pl.ds(g * bx, bx)
    their_x = pl.ds((1 - g) * bx, bx)
    partner = xi + 1 - 2 * g
    loads = [
        pltpu.make_async_copy(ref.at[mine_x], f1.at[q, own_x, own_y, mine_z], load_sem.at[q])
        for q, ref in ((0, coef_ref), (1, rhs_ref))
    ]
    for copy in loads:
        copy.start()
    for q in (0, 1):
        for p in (0, n3 + 1):
            f3[q, p] = jnp.zeros(f3.shape[2:], F32)
        for p in (0, n4 + 1):
            f4[q, p] = jnp.zeros(f4.shape[2:], F32)
    for k in range(FINE_DEGREE):
        for p in (0, n3 + 1):
            d3[k, p] = jnp.zeros(d3.shape[2:], F32)
    for k in range(2):
        for p in (0, n4 + 1):
            d4[k, p] = jnp.zeros(d4.shape[2:], F32)

    around = [(dx, dy) for dx in range(-2, 3) for dy in range(-1, 2) if (dx, dy) != (0, 0)]
    close = [(dx, dy) for dx, dy in around if abs(dx) < 2]

    barrier = pltpu.get_barrier_semaphore()
    for dx, dy in around:

        @pl.when(valid(dx, dy))
        def _(dx=dx, dy=dy):
            pl.semaphore_signal(barrier, 1, device_id=where_is(xi + dx, gy + dy), device_id_type=MESH)

    for o in range(1, gy_size):
        pl.semaphore_signal(barrier, 1, device_id=where_is(xi, lax.rem(gy + o, gy_size)), device_id_type=MESH)
    for o in range(1, nx):
        pl.semaphore_signal(barrier, 1, device_id=where_is(lax.rem(xi + o, nx), gy), device_id_type=MESH)
    count_x = 1 + sum(jnp.where((xi + dx >= 0) & (xi + dx < nx), 1, 0) for dx in (-2, -1, 1, 2))
    count_y = 1 + sum(jnp.where((gy + dy >= 0) & (gy + dy < gy_size), 1, 0) for dy in (-1, 1))
    pl.semaphore_wait(barrier, count_x * count_y - 1 + gy_size - 1 + nx - 1)

    swaps = [
        remote(ref.at[their_x], f1.at[q, own_x, own_y, mine_z], pair_send.at[q], pair_recv.at[q], partner, gy)
        for q, ref in ((0, coef_ref), (1, rhs_ref))
    ]
    for copy in swaps:
        copy.start()
    arrivals = [
        remote(ref.at[their_x], f1.at[q, own_x, own_y, their_z], pair_send.at[q], pair_recv.at[q], partner, gy)
        for q, ref in ((0, coef_ref), (1, rhs_ref))
    ]
    for copy in swaps:
        copy.wait_send()
    for copy in arrivals:
        copy.wait_recv()
    for copy in loads:
        copy.wait()

    half_z_mat = pick(lanes1, lanes, lambda i, j: (i >> 1) == j, 0.125)
    half_z2 = pick(lanes, lanes, lambda i, j: (i >> 1) == j, 0.125)
    twice_z = pick(lanes, lanes, lambda i, j: (j >> 1) == i)
    twice_z1 = pick(lanes, lanes1, lambda i, j: (j >> 1) == i)
    rows1, rows2 = f1.shape[2], f2.shape[2]
    b3 = b2 // 2

    def blocks(count, rows, columns, rule):
        def whole(i, j):
            found = False
            for r in range(count):
                a, b = i - r * rows, j - r * columns
                found = found | ((a >= 0) & (a < rows) & (b >= 0) & (b < columns) & rule(a, b))
            return found

        return pick(count * rows, count * columns, whole)

    twice_y2 = blocks(b3 + 2, rows2, y3, lambda i, j: ((gy * y2 - 8 + i) >> 1) == j)
    twice_y1 = blocks(b2 + 2, rows1, rows2, lambda i, j: (i >> 1) + 4 == j)
    first_half = lax.broadcasted_iota(jnp.int32, (8, lanes), 1) < lanes // 2
    upper = lax.broadcasted_iota(jnp.int32, (8, lanes), 0) < 4

    def pairs(value):
        n = value.shape[0]
        tmp[0:n] = value
        return tmp[pl.ds(0, n // 2, 2)] + tmp[pl.ds(1, n // 2, 2)]

    fine = cheb_steps(FINE_DEGREE, LOW_FINE, HIGH_BOUND)
    coarse = cheb_steps(COARSE_DEGREE, LOW_COARSE, HIGH_BOUND)

    for outer in range(OUTER):
        q0, count = ((0, 2), (2, 1))[outer]
        qs = pl.ds(q0, count)
        now = q0 + count - 1

        copies1 = []
        for k, (dx, dy) in enumerate(close):
            h = H1 - outer - (1 if dy else 0)
            src_x, dst_x = {
                0: (own_x, own_x),
                1: (pl.ds(H1 + bx - h, h), pl.ds(H1 - h, h)),
                -1: (pl.ds(H1, h), pl.ds(H1 + bx, h)),
            }[dx]
            src_y, dst_y = {
                0: (own_y, own_y),
                1: (pl.ds(by, 8), pl.ds(0, 8)),
                -1: (pl.ds(8, 8), pl.ds(8 + by, 8)),
            }[dy]
            copies1.append((dx, dy, remote(
                f1.at[qs, src_x, src_y], f1.at[qs, dst_x, dst_y],
                s1_send.at[outer, k], s1_recv.at[outer, k], xi + dx, gy + dy,
            )))
        copies2 = []
        for k, (dx, dy) in enumerate(around):
            if outer and abs(dx) == 2 and dy:
                continue
            copies2.append((dx, dy, remote(
                f2.at[qs, pl.ds(2 * b2, b2), pl.ds(8, y2)],
                f2.at[qs, pl.ds(2 * b2 - b2 * dx, b2), pl.ds(8 - y2 * dy, y2)],
                s2_send.at[outer, k], s2_recv.at[outer, k], xi + dx, gy + dy,
            )))

        def start(copies):
            for dx, dy, copy in copies:
                pl.when(valid(dx, dy))(copy.start)

        def finish(copies):
            for dx, dy, copy in copies:
                pl.when(valid(-dx, -dy))(copy.wait_recv)

        def drain(copies):
            for dx, dy, copy in copies:
                pl.when(valid(dx, dy))(copy.wait_send)

        parts = [
            f1[q, H1 + 2 * p, 8 : 8 + by] + f1[q, H1 + 2 * p + 1, 8 : 8 + by]
            for q in range(q0, q0 + count) for p in range(b2)
        ]
        halves = pairs(dot(jnp.concatenate(parts, axis=0), half_z_mat))
        parts = [halves[k * y2 : (k + 1) * y2] for k in range(count * b2)]
        for k in range(count * b2):
            f2[q0 + k // b2, 2 * b2 + k % b2, 8 : 8 + y2] = parts[k]
        start(copies2)
        parts = [parts[2 * k] + parts[2 * k + 1] for k in range(count * b3)]
        halves = pairs(dot(jnp.concatenate(parts, axis=0), half_z2))
        if count == 2:
            gath[outer, xi, gy] = halves[0:8] + pltpu.roll(halves[8:16], lanes // 2, 1)
        else:
            gath[outer, xi, gy] = halves

        def along_y(o):
            return remote(
                gath.at[outer, xi, gy], gath.at[outer, xi, gy],
                gy_send.at[outer, o], gy_recv.at[outer, o], xi, lax.rem(gy + o, gy_size),
            )

        def from_y(o):
            y = lax.rem(gy + gy_size - o, gy_size)
            return remote(
                gath.at[outer, xi, y], gath.at[outer, xi, y],
                gy_send.at[outer, o], gy_recv.at[outer, o], xi, lax.rem(gy + o, gy_size),
            )

        def along_x(o):
            return remote(
                gath.at[outer, xi], gath.at[outer, xi],
                gx_send.at[outer, o], gx_recv.at[outer, o], lax.rem(xi + o, nx), gy,
            )

        def from_x(o):
            x = lax.rem(xi + nx - o, nx)
            return remote(
                gath.at[outer, x], gath.at[outer, x],
                gx_send.at[outer, o], gx_recv.at[outer, o], lax.rem(xi + o, nx), gy,
            )

        for o in range(1, gy_size):
            along_y(o).start()
        for o in range(1, gy_size):
            from_y(o).wait_recv()
        for o in range(1, nx):
            along_x(o).start()

        start(copies1)
        finish(copies2)
        low, high = 2 * b2 - 5, 3 * b2 + 5
        if outer == 0:
            build(f2.at[0], w2, inv2, low, high, 4)
        first_update(f2.at[now], inv2, t2, d2.at[0], 0.25, fine[0], low, high, 16)
        for k in range(FINE_DEGREE - 1):
            low, high = low + 1, high - 1
            advance(w2, t2, d2.at[k], d2.at[k + 1], fine[1][k], fine[2][k], low, high, 16)

        for o in range(1, nx):
            from_x(o).wait_recv()
        def unpack(x):
            for k in range(gy_size // 2):
                even, odd = gath[outer, x, 2 * k], gath[outer, x, 2 * k + 1]
                place = slice(8 * k, 8 * k + 8)
                one = jnp.where(upper, even, pltpu.roll(odd, 4, 0))
                two = jnp.where(upper, pltpu.roll(even, 4, 0), odd)
                for p, value in ((1 + 2 * x, one), (2 + 2 * x, two)):
                    if count == 2:
                        f3[0, p, place] = jnp.where(first_half, value, 0.0)
                        value = jnp.where(first_half, pltpu.roll(value, lanes // 2, 1), 0.0)
                    f3[1, p, place] = value

        loop(0, nx, unpack, 8)

        slots = (0, 1) if count == 2 else (1,)
        parts = [f3[slot, 1 + 2 * x] + f3[slot, 2 + 2 * x] for slot in slots for x in range(n4)]
        halves = pairs(dot(jnp.concatenate(parts, axis=0), half_z2))
        for k in range(count * n4):
            f4[slots[k // n4], 1 + k % n4] = halves[k * y4 : (k + 1) * y4]
        if outer == 0:
            build(f4.at[0], w4, inv4, 1, n4 + 1, 8)
            build(f3.at[0], w3, inv3, 1, n3 + 1, 4)
        small = n4 * y4 <= 64
        width = 16 if small else 4
        first_update(f4.at[1], inv4, t4, d4.at[0], 0.015625, coarse[0], 1, n4 + 1, 8)
        first_update(f3.at[1], inv3, t3, d3.at[0], 0.0625, fine[0], 1, n3 + 1, width)
        if small:
            zero = jnp.zeros((y4, lanes), F32)
            vs = [d4[0, 1 + p] for p in range(n4)]
            ts = [t4[1 + p] for p in range(n4)]
            sums = list(vs)
        else:

            def begin4(p):
                c4[p] = d4[0, p]

            loop(1, n4 + 1, begin4, 8)
        for k in range(COARSE_DEGREE - 1):
            if small:
                edged = [zero] + vs + [zero]
                news = []
                for p in range(n4):
                    c = vs[p]
                    acc = w4[0, 1 + p] * edged[p] + w4[1, 1 + p] * edged[p + 2]
                    acc2 = w4[2, 1 + p] * pltpu.roll(c, 1, 0) + w4[3, 1 + p] * pltpu.roll(c, y4 - 1, 0)
                    acc3 = w4[4, 1 + p] * pltpu.roll(c, 1, 1) + w4[5, 1 + p] * pltpu.roll(c, lanes - 1, 1)
                    ts[p] = ts[p] - c + (acc + (acc2 + acc3))
                    news.append(coarse[1][k] * c + coarse[2][k] * ts[p])
                    sums[p] = sums[p] + news[p]
                vs = news
            else:
                advance(w4, t4, d4.at[k % 2], d4.at[(k + 1) % 2], coarse[1][k], coarse[2][k], 1, n4 + 1, 8, c4)
            if k % 3 == 0 and k // 3 < FINE_DEGREE - 1:
                m = k // 3
                advance(w3, t3, d3.at[m], d3.at[m + 1], fine[1][m], fine[2][m], 1, n3 + 1, width)
        if small:
            for p in range(n4):
                c4[1 + p] = sums[p]

        wide = dot(jnp.concatenate([c4[1 + x] for x in range(n4)], axis=0), twice_z)
        tmp[pl.ds(0, n4 * y4, 2)] = wide
        tmp[pl.ds(1, n4 * y4, 2)] = wide
        for x in range(n4):
            add = tmp[x * y3 : (x + 1) * y3]
            for p in (1 + 2 * x, 2 + 2 * x):
                c3[p] = ((d3[0, p] + d3[1, p]) + (d3[2, p] + d3[3, p])) + d3[4, p] + add
        parts = [c3[jnp.clip(xi * b3 + r, 0, n3 - 1) + 1] for r in range(-1, b3 + 1)]
        wide = dot(twice_y2, dot(jnp.concatenate(parts, axis=0), twice_z))
        for r in range(-1, b3 + 1):
            add = wide[(r + 1) * rows2 : (r + 2) * rows2]
            for p in (2 * b2 + 2 * r, 2 * b2 + 2 * r + 1):
                if 2 * b2 - 1 <= p < 3 * b2 + 1:
                    c2[p] = ((d2[0, p] + d2[1, p]) + (d2[2, p] + d2[3, p])) + d2[4, p] + add
        parts = [c2[2 * b2 + r] for r in range(-1, b2 + 1)]
        wide1 = dot(twice_y1, dot(jnp.concatenate(parts, axis=0), twice_z1))
        for r in range(b2 + 2):
            c1[r] = wide1[r * rows1 : (r + 1) * rows1]

        finish(copies1)
        low, high = H1 - 5, H1 + bx + 5
        if outer == 0:
            build(f1.at[0], w1, inv1, low, high, 1, diag1)
        first_update(f1.at[now], inv1, t1, d1.at[0], 1.0, fine[0], low, high, 2)
        for k in range(FINE_DEGREE - 1):
            low, high = low + 1, high - 1
            advance(w1, t1, d1.at[k], d1.at[k + 1], fine[1][k], fine[2][k], low, high, 4)

        for r in range(-1, b2 + 1):
            add = c1[r + 1]
            for p in (H1 + 2 * r, H1 + 2 * r + 1):
                if H1 - 1 <= p < H1 + bx + 1:
                    both = ((d1[0, p] + d1[1, p]) + (d1[2, p] + d1[3, p])) + d1[4, p] + add
                    if outer == 0:
                        u1[p] = DAMPING * both
                    else:
                        u1[p] = u1[p] + DAMPING * both

        def leftover(p):
            c, acc = nearby(w1, u1, p)
            value = f1[1, p] - diag1[p] * (c - acc)
            if outer + 1 < OUTER:
                f1[2, p, 8 : 8 + by] = value[8 : 8 + by]
            else:
                last[p - H1] = value[8 : 8 + by]

        loop(H1, H1 + bx, leftover, 2)
        drain(copies1)
        drain(copies2)
        for o in range(1, gy_size):
            along_y(o).wait_send()
        for o in range(1, nx):
            along_x(o).wait_send()

    outs = [
        remote(u1.at[own_x, own_y, their_z], sol_ref.at[mine_x], out_send.at[0], out_recv.at[0], partner, gy),
        remote(last.at[:, :, their_z], res_ref.at[mine_x], out_send.at[1], out_recv.at[1], partner, gy),
    ]
    for copy in outs:
        copy.start()
    sol_ref[mine_x] = u1[own_x, own_y, mine_z]
    res_ref[mine_x] = last[:, :, mine_z]
    for copy in outs:
        copy.wait_send()
    remote(u1.at[own_x, own_y, their_z], sol_ref.at[their_x], out_send.at[0], out_recv.at[0], partner, gy).wait_recv()
    remote(last.at[:, :, their_z], res_ref.at[their_x], out_send.at[1], out_recv.at[1], partner, gy).wait_recv()


def solution(mesh):
    gx_size, gy_size = mesh.shape["gx"], mesh.shape["gy"]

    def on_device(right_side, coefficient):
        full_x, by, half_z = right_side.shape
        bx = full_x // 2
        nx = 2 * gx_size
        lanes = half_z
        p1, r1, l1 = bx + 2 * H1, by + 16, 2 * half_z
        b2, y2 = bx // 2, by // 2
        p2, r2 = 5 * b2, y2 + 16
        p3, r3 = nx * bx // 4 + 2, gy_size * by // 4
        p4, r4 = nx * bx // 8 + 2, gy_size * by // 8
        vm = lambda *shape: pltpu.VMEM(shape, F32)
        sem = lambda *shape: pltpu.SemaphoreType.DMA(shape)
        return pl.pallas_call(
            functools.partial(kernel, gx_size, gy_size),
            out_shape=(jax.ShapeDtypeStruct(right_side.shape, F32),) * 2,
            in_specs=[pl.BlockSpec(memory_space=pltpu.HBM)] * 2,
            out_specs=(pl.BlockSpec(memory_space=pltpu.VMEM),) * 2,
            scratch_shapes=[
                vm(3, p1, r1, l1), vm(6, p1, r1, l1), vm(p1, r1, l1), vm(p1, r1, l1), vm(p1, r1, l1),
                vm(FINE_DEGREE, p1, r1, l1), vm(p1, r1, l1), vm(bx, by, l1),
                vm(3, p2, r2, lanes), vm(6, p2, r2, lanes), vm(p2, r2, lanes), vm(p2, r2, lanes),
                vm(FINE_DEGREE, p2, r2, lanes), vm(p2, r2, lanes),
                vm(2, nx, gy_size, 8, lanes),
                vm(2, p3, r3, lanes), vm(6, p3, r3, lanes), vm(p3, r3, lanes), vm(p3, r3, lanes),
                vm(FINE_DEGREE, p3, r3, lanes), vm(p3, r3, lanes),
                vm(2, p4, r4, lanes), vm(6, p4, r4, lanes), vm(p4, r4, lanes), vm(p4, r4, lanes),
                vm(2, p4, r4, lanes), vm(p4, r4, lanes),
                vm(max((p3 - 2) * r3, 2 * b2 * by), lanes), vm(b2 + 2, r1, l1), sem(2),
                sem(2), sem(2), sem(2, 8), sem(2, 8), sem(2, 14), sem(2, 14),
                sem(2, gy_size), sem(2, gy_size), sem(2, nx), sem(2, nx), sem(2), sem(2),
            ],
            compiler_params=pltpu.CompilerParams(
                collective_id=0, has_side_effects=True, vmem_limit_bytes=64 * 1024 * 1024
            ),
        )(right_side, coefficient)

    placed = (P("gx", "gy", "grp"), P("gx", "gy", "grp"))
    return jax.shard_map(on_device, mesh=mesh, in_specs=placed, out_specs=placed, check_vma=False)
```

```python
import functools

import jax
import jax.numpy as jnp
from jax import lax
from jax.experimental import pallas as pl
from jax.experimental.pallas import tpu as pltpu
from jax.sharding import PartitionSpec as P

FINE_DEGREE = 5
COARSE_DEGREE = 16
OUTER = 2
LOW_FINE = 0.2
LOW_COARSE = 0.02
HIGH_BOUND = 2.0
DAMPING = 0.5
H1 = 6
MESH = pl.DeviceIdType.MESH
F32 = jnp.float32


def cheb_steps(degree, low, high):
    theta = (high + low) / 2.0
    delta = (high - low) / 2.0
    sigma = theta / delta
    rho = 1.0 / sigma
    keeps = []
    pushes = []
    for step in range(degree - 1):
        rho_new = 1.0 / (2.0 * sigma - rho)
        keeps.append(rho_new * rho)
        pushes.append(2.0 * rho_new / delta)
        rho = rho_new
    return (1.0 / theta, keeps, pushes)


def dot(a, b):
    def times(x, y):
        return jnp.dot(x, y, preferred_element_type=F32)

    if a.dtype == jnp.bfloat16:
        top, middle, rest = thirds(b)
        return times(a, top) + (times(a, middle) + times(a, rest))
    top, middle, rest = thirds(a)
    return times(top, b) + (times(middle, b) + times(rest, b))


def thirds(x):
    top = x.astype(jnp.bfloat16)
    left = x - top.astype(F32)
    middle = left.astype(jnp.bfloat16)
    return top, middle, (left - middle.astype(F32)).astype(jnp.bfloat16)


def loop(low, high, body, unroll):
    whole = (high - low) // unroll
    if whole > 1:

        def several(i, carry):
            for j in range(unroll):
                body(low + i * unroll + j)
            return carry

        lax.fori_loop(0, whole, several, 0)
    else:
        whole = 0
    for p in range(low + whole * unroll, high):
        body(p)


def pick(rows, columns, rule, value=1.0):
    i = lax.broadcasted_iota(jnp.int32, (rows, columns), 0)
    j = lax.broadcasted_iota(jnp.int32, (rows, columns), 1)
    return jnp.where(rule(i, j), value, 0.0).astype(jnp.bfloat16)


def build(a, w, inv, low, high, unroll, diag=None):
    rows, lanes = a.shape[-2:]
    i = lax.broadcasted_iota(jnp.int32, (rows, lanes), 0)
    j = lax.broadcasted_iota(jnp.int32, (rows, lanes), 1)

    def body(p):
        c = a[p]
        near = (
            a[p - 1],
            a[p + 1],
            jnp.where(i == 0, 0.0, pltpu.roll(c, 1, 0)),
            jnp.where(i == rows - 1, 0.0, pltpu.roll(c, rows - 1, 0)),
            jnp.where(j == 0, 0.0, pltpu.roll(c, 1, 1)),
            jnp.where(j == lanes - 1, 0.0, pltpu.roll(c, lanes - 1, 1)),
        )
        faces = [0.5 * (c + n) for n in near]
        total = faces[0] + faces[1] + faces[2] + faces[3] + faces[4] + faces[5]
        good = c > 0.0
        inverse = jnp.where(good, 1.0 / jnp.where(good, total, 1.0), 0.0)
        inv[p] = inverse
        if diag is not None:
            diag[p] = total
        for k in range(6):
            w[k, p] = jnp.where(near[k] > 0.0, faces[k] * inverse, 0.0)

    loop(low, high, body, unroll)


def nearby(w, v, p):
    c = v[p]
    rows, lanes = c.shape
    acc = w[0, p] * v[p - 1] + w[1, p] * v[p + 1]
    acc2 = w[2, p] * pltpu.roll(c, 1, 0) + w[3, p] * pltpu.roll(c, rows - 1, 0)
    acc3 = w[4, p] * pltpu.roll(c, 1, 1) + w[5, p] * pltpu.roll(c, lanes - 1, 1)
    return c, acc + (acc2 + acc3)


def first_update(r, inv, t, d, scale, inv_theta, low, high, unroll):
    def body(p):
        start = r[p] * inv[p] * (1.0 / scale)
        t[p] = start
        d[p] = start * inv_theta

    loop(low, high, body, unroll)


def advance(w, t, d, d_next, keep, push, low, high, unroll, total=None):
    def body(p):
        c, acc = nearby(w, d, p)
        left = t[p] - c + acc
        t[p] = left
        new = keep * c + push * left
        d_next[p] = new
        if total is not None:
            total[p] = total[p] + new

    loop(low, high, body, unroll)


def kernel(
    gx_size, gy_size,
    rhs_ref, coef_ref, sol_ref, res_ref,
    f1, w1, inv1, diag1, t1, d1, u1, last,
    f2, w2, inv2, t2, d2, c2,
    gath, f3, w3, inv3, t3, d3, c3,
    f4, w4, inv4, t4, d4, c4,
    tmp, c1, load_sem,
    pair_send, pair_recv, s1_send, s1_recv, s2_send, s2_recv, gy_send, gy_recv, gx_send, gx_recv,
    out_send, out_recv,
):
    g = lax.axis_index("grp")
    gy = lax.axis_index("gy")
    nx = 2 * gx_size
    xi = 2 * lax.axis_index("gx") + g
    full_x, by, half_z = rhs_ref.shape
    bx = full_x // 2
    lanes1 = 2 * half_z
    lanes = half_z
    y2, y3, y4 = by // 2, f3.shape[2], f4.shape[2]
    b2 = bx // 2
    n3, n4 = f3.shape[1] - 2, f4.shape[1] - 2

    def where_is(x, y):
        return {"grp": lax.rem(x, 2), "gx": lax.div(x, 2), "gy": y}

    def valid(dx, dy):
        x, y = xi + dx, gy + dy
        return (x >= 0) & (x < nx) & (y >= 0) & (y < gy_size)

    def remote(src, dst, send, recv, x, y):
        return pltpu.make_async_remote_copy(
            src_ref=src, dst_ref=dst, send_sem=send, recv_sem=recv,
            device_id=where_is(x, y), device_id_type=MESH,
        )

    def clear1(p):
        for q in range(3):
            f1[q, p] = jnp.zeros(f1.shape[2:], F32)

    loop(0, f1.shape[1], clear1, 1)

    def clear2(p):
        for q in range(3):
            f2[q, p] = jnp.zeros(f2.shape[2:], F32)

    loop(0, f2.shape[1], clear2, 2)
    own_x = pl.ds(H1, bx)
    own_y = pl.ds(8, by)
    mine_z = pl.ds(pl.multiple_of(g * half_z, half_z), half_z)
    their_z = pl.ds(pl.multiple_of((1 - g) * half_z, half_z), half_z)
    mine_x = pl.ds(g * bx, bx)
    their_x = pl.ds((1 - g) * bx, bx)
    partner = xi + 1 - 2 * g
    loads = [
        pltpu.make_async_copy(ref.at[mine_x], f1.at[q, own_x, own_y, mine_z], load_sem.at[q])
        for q, ref in ((0, coef_ref), (1, rhs_ref))
    ]
    for copy in loads:
        copy.start()
    for q in (0, 1):
        for p in (0, n3 + 1):
            f3[q, p] = jnp.zeros(f3.shape[2:], F32)
        for p in (0, n4 + 1):
            f4[q, p] = jnp.zeros(f4.shape[2:], F32)
    for k in range(FINE_DEGREE):
        for p in (0, n3 + 1):
            d3[k, p] = jnp.zeros(d3.shape[2:], F32)
    for k in range(2):
        for p in (0, n4 + 1):
            d4[k, p] = jnp.zeros(d4.shape[2:], F32)

    around = [(dx, dy) for dx in range(-2, 3) for dy in range(-1, 2) if (dx, dy) != (0, 0)]
    close = [(dx, dy) for dx, dy in around if abs(dx) < 2]

    barrier = pltpu.get_barrier_semaphore()
    for dx, dy in around:

        @pl.when(valid(dx, dy))
        def _(dx=dx, dy=dy):
            pl.semaphore_signal(barrier, 1, device_id=where_is(xi + dx, gy + dy), device_id_type=MESH)

    for o in range(1, gy_size):
        pl.semaphore_signal(barrier, 1, device_id=where_is(xi, lax.rem(gy + o, gy_size)), device_id_type=MESH)
    for o in range(1, nx):
        pl.semaphore_signal(barrier, 1, device_id=where_is(lax.rem(xi + o, nx), gy), device_id_type=MESH)
    count_x = 1 + sum(jnp.where((xi + dx >= 0) & (xi + dx < nx), 1, 0) for dx in (-2, -1, 1, 2))
    count_y = 1 + sum(jnp.where((gy + dy >= 0) & (gy + dy < gy_size), 1, 0) for dy in (-1, 1))
    pl.semaphore_wait(barrier, count_x * count_y - 1 + gy_size - 1 + nx - 1)

    swaps = [
        remote(ref.at[their_x], f1.at[q, own_x, own_y, mine_z], pair_send.at[q], pair_recv.at[q], partner, gy)
        for q, ref in ((0, coef_ref), (1, rhs_ref))
    ]
    for copy in swaps:
        copy.start()
    arrivals = [
        remote(ref.at[their_x], f1.at[q, own_x, own_y, their_z], pair_send.at[q], pair_recv.at[q], partner, gy)
        for q, ref in ((0, coef_ref), (1, rhs_ref))
    ]
    for copy in swaps:
        copy.wait_send()
    for copy in arrivals:
        copy.wait_recv()
    for copy in loads:
        copy.wait()

    half_z_mat = pick(lanes1, lanes, lambda i, j: (i >> 1) == j, 0.125)
    half_z2 = pick(lanes, lanes, lambda i, j: (i >> 1) == j, 0.125)
    twice_z = pick(lanes, lanes, lambda i, j: (j >> 1) == i)
    twice_z1 = pick(lanes, lanes1, lambda i, j: (j >> 1) == i)
    rows1, rows2 = f1.shape[2], f2.shape[2]
    b3 = b2 // 2

    def blocks(count, rows, columns, rule):
        def whole(i, j):
            found = False
            for r in range(count):
                a, b = i - r * rows, j - r * columns
                found = found | ((a >= 0) & (a < rows) & (b >= 0) & (b < columns) & rule(a, b))
            return found

        return pick(count * rows, count * columns, whole)

    twice_y2 = blocks(b3 + 2, rows2, y3, lambda i, j: ((gy * y2 - 8 + i) >> 1) == j)
    twice_y1 = blocks(b2 + 2, rows1, rows2, lambda i, j: (i >> 1) + 4 == j)
    first_half = lax.broadcasted_iota(jnp.int32, (8, lanes), 1) < lanes // 2
    upper = lax.broadcasted_iota(jnp.int32, (8, lanes), 0) < 4

    def pairs(value):
        n = value.shape[0]
        tmp[0:n] = value
        return tmp[pl.ds(0, n // 2, 2)] + tmp[pl.ds(1, n // 2, 2)]

    fine = cheb_steps(FINE_DEGREE, LOW_FINE, HIGH_BOUND)
    coarse = cheb_steps(COARSE_DEGREE, LOW_COARSE, HIGH_BOUND)

    for outer in range(OUTER):
        q0, count = ((0, 2), (2, 1))[outer]
        qs = pl.ds(q0, count)
        now = q0 + count - 1

        copies1 = []
        for k, (dx, dy) in enumerate(close):
            h = H1 - outer - (1 if dy else 0)
            src_x, dst_x = {
                0: (own_x, own_x),
                1: (pl.ds(H1 + bx - h, h), pl.ds(H1 - h, h)),
                -1: (pl.ds(H1, h), pl.ds(H1 + bx, h)),
            }[dx]
            src_y, dst_y = {
                0: (own_y, own_y),
                1: (pl.ds(by, 8), pl.ds(0, 8)),
                -1: (pl.ds(8, 8), pl.ds(8 + by, 8)),
            }[dy]
            copies1.append((dx, dy, remote(
                f1.at[qs, src_x, src_y], f1.at[qs, dst_x, dst_y],
                s1_send.at[outer, k], s1_recv.at[outer, k], xi + dx, gy + dy,
            )))
        copies2 = []
        for k, (dx, dy) in enumerate(around):
            if outer and abs(dx) == 2 and dy:
                continue
            copies2.append((dx, dy, remote(
                f2.at[qs, pl.ds(2 * b2, b2), pl.ds(8, y2)],
                f2.at[qs, pl.ds(2 * b2 - b2 * dx, b2), pl.ds(8 - y2 * dy, y2)],
                s2_send.at[outer, k], s2_recv.at[outer, k], xi + dx, gy + dy,
            )))

        def start(copies):
            for dx, dy, copy in copies:
                pl.when(valid(dx, dy))(copy.start)

        def finish(copies):
            for dx, dy, copy in copies:
                pl.when(valid(-dx, -dy))(copy.wait_recv)

        def drain(copies):
            for dx, dy, copy in copies:
                pl.when(valid(dx, dy))(copy.wait_send)

        parts = [
            f1[q, H1 + 2 * p, 8 : 8 + by] + f1[q, H1 + 2 * p + 1, 8 : 8 + by]
            for q in range(q0, q0 + count) for p in range(b2)
        ]
        halves = pairs(dot(jnp.concatenate(parts, axis=0), half_z_mat))
        parts = [halves[k * y2 : (k + 1) * y2] for k in range(count * b2)]
        for k in range(count * b2):
            f2[q0 + k // b2, 2 * b2 + k % b2, 8 : 8 + y2] = parts[k]
        start(copies2)
        parts = [parts[2 * k] + parts[2 * k + 1] for k in range(count * b3)]
        halves = pairs(dot(jnp.concatenate(parts, axis=0), half_z2))
        if count == 2:
            gath[outer, xi, gy] = halves[0:8] + pltpu.roll(halves[8:16], lanes // 2, 1)
        else:
            gath[outer, xi, gy] = halves

        def along_y(o):
            return remote(
                gath.at[outer, xi, gy], gath.at[outer, xi, gy],
                gy_send.at[outer, o], gy_recv.at[outer, o], xi, lax.rem(gy + o, gy_size),
            )

        def from_y(o):
            y = lax.rem(gy + gy_size - o, gy_size)
            return remote(
                gath.at[outer, xi, y], gath.at[outer, xi, y],
                gy_send.at[outer, o], gy_recv.at[outer, o], xi, lax.rem(gy + o, gy_size),
            )

        def along_x(o):
            return remote(
                gath.at[outer, xi], gath.at[outer, xi],
                gx_send.at[outer, o], gx_recv.at[outer, o], lax.rem(xi + o, nx), gy,
            )

        def from_x(o):
            x = lax.rem(xi + nx - o, nx)
            return remote(
                gath.at[outer, x], gath.at[outer, x],
                gx_send.at[outer, o], gx_recv.at[outer, o], lax.rem(xi + o, nx), gy,
            )

        for o in range(1, gy_size):
            along_y(o).start()
        for o in range(1, gy_size):
            from_y(o).wait_recv()
        for o in range(1, nx):
            along_x(o).start()

        start(copies1)
        finish(copies2)
        low, high = 2 * b2 - 5, 3 * b2 + 5
        if outer == 0:
            build(f2.at[0], w2, inv2, low, high, 4)
        first_update(f2.at[now], inv2, t2, d2.at[0], 0.25, fine[0], low, high, 16)
        for k in range(FINE_DEGREE - 1):
            low, high = low + 1, high - 1
            advance(w2, t2, d2.at[k], d2.at[k + 1], fine[1][k], fine[2][k], low, high, 16)

        for o in range(1, nx):
            from_x(o).wait_recv()
        def unpack(x):
            for k in range(gy_size // 2):
                even, odd = gath[outer, x, 2 * k], gath[outer, x, 2 * k + 1]
                place = slice(8 * k, 8 * k + 8)
                one = jnp.where(upper, even, pltpu.roll(odd, 4, 0))
                two = jnp.where(upper, pltpu.roll(even, 4, 0), odd)
                for p, value in ((1 + 2 * x, one), (2 + 2 * x, two)):
                    if count == 2:
                        f3[0, p, place] = jnp.where(first_half, value, 0.0)
                        value = jnp.where(first_half, pltpu.roll(value, lanes // 2, 1), 0.0)
                    f3[1, p, place] = value

        loop(0, nx, unpack, 8)

        slots = (0, 1) if count == 2 else (1,)
        parts = [f3[slot, 1 + 2 * x] + f3[slot, 2 + 2 * x] for slot in slots for x in range(n4)]
        halves = pairs(dot(jnp.concatenate(parts, axis=0), half_z2))
        for k in range(count * n4):
            f4[slots[k // n4], 1 + k % n4] = halves[k * y4 : (k + 1) * y4]
        if outer == 0:
            build(f4.at[0], w4, inv4, 1, n4 + 1, 8)
            build(f3.at[0], w3, inv3, 1, n3 + 1, 4)
        small = n4 * y4 <= 64
        width = 16 if small else 4
        first_update(f4.at[1], inv4, t4, d4.at[0], 0.015625, coarse[0], 1, n4 + 1, 8)
        first_update(f3.at[1], inv3, t3, d3.at[0], 0.0625, fine[0], 1, n3 + 1, width)
        if small:
            zero = jnp.zeros((y4, lanes), F32)
            vs = [d4[0, 1 + p] for p in range(n4)]
            ts = [t4[1 + p] for p in range(n4)]
            sums = list(vs)
        else:

            def begin4(p):
                c4[p] = d4[0, p]

            loop(1, n4 + 1, begin4, 8)
        for k in range(COARSE_DEGREE - 1):
            if small:
                edged = [zero] + vs + [zero]
                news = []
                for p in range(n4):
                    c = vs[p]
                    acc = w4[0, 1 + p] * edged[p] + w4[1, 1 + p] * edged[p + 2]
                    acc2 = w4[2, 1 + p] * pltpu.roll(c, 1, 0) + w4[3, 1 + p] * pltpu.roll(c, y4 - 1, 0)
                    acc3 = w4[4, 1 + p] * pltpu.roll(c, 1, 1) + w4[5, 1 + p] * pltpu.roll(c, lanes - 1, 1)
                    ts[p] = ts[p] - c + (acc + (acc2 + acc3))
                    news.append(coarse[1][k] * c + coarse[2][k] * ts[p])
                    sums[p] = sums[p] + news[p]
                vs = news
            else:
                advance(w4, t4, d4.at[k % 2], d4.at[(k + 1) % 2], coarse[1][k], coarse[2][k], 1, n4 + 1, 8, c4)
            if k % 3 == 0 and k // 3 < FINE_DEGREE - 1:
                m = k // 3
                advance(w3, t3, d3.at[m], d3.at[m + 1], fine[1][m], fine[2][m], 1, n3 + 1, width)
        if small:
            for p in range(n4):
                c4[1 + p] = sums[p]

        wide = dot(jnp.concatenate([c4[1 + x] for x in range(n4)], axis=0), twice_z)
        tmp[pl.ds(0, n4 * y4, 2)] = wide
        tmp[pl.ds(1, n4 * y4, 2)] = wide
        for x in range(n4):
            add = tmp[x * y3 : (x + 1) * y3]
            for p in (1 + 2 * x, 2 + 2 * x):
                c3[p] = ((d3[0, p] + d3[1, p]) + (d3[2, p] + d3[3, p])) + d3[4, p] + add
        parts = [c3[jnp.clip(xi * b3 + r, 0, n3 - 1) + 1] for r in range(-1, b3 + 1)]
        wide = dot(twice_y2, dot(jnp.concatenate(parts, axis=0), twice_z))
        for r in range(-1, b3 + 1):
            add = wide[(r + 1) * rows2 : (r + 2) * rows2]
            for p in (2 * b2 + 2 * r, 2 * b2 + 2 * r + 1):
                if 2 * b2 - 1 <= p < 3 * b2 + 1:
                    c2[p] = ((d2[0, p] + d2[1, p]) + (d2[2, p] + d2[3, p])) + d2[4, p] + add
        parts = [c2[2 * b2 + r] for r in range(-1, b2 + 1)]
        wide1 = dot(twice_y1, dot(jnp.concatenate(parts, axis=0), twice_z1))
        for r in range(b2 + 2):
            c1[r] = wide1[r * rows1 : (r + 1) * rows1]

        finish(copies1)
        low, high = H1 - 5, H1 + bx + 5
        if outer == 0:
            build(f1.at[0], w1, inv1, low, high, 3, diag1)
        first_update(f1.at[now], inv1, t1, d1.at[0], 1.0, fine[0], low, high, 6)
        for k in range(FINE_DEGREE - 1):
            low, high = low + 1, high - 1
            advance(w1, t1, d1.at[k], d1.at[k + 1], fine[1][k], fine[2][k], low, high, (high - low) // 2)

        for r in range(-1, b2 + 1):
            add = c1[r + 1]
            for p in (H1 + 2 * r, H1 + 2 * r + 1):
                if H1 - 1 <= p < H1 + bx + 1:
                    both = ((d1[0, p] + d1[1, p]) + (d1[2, p] + d1[3, p])) + d1[4, p] + add
                    if outer == 0:
                        u1[p] = DAMPING * both
                    else:
                        u1[p] = u1[p] + DAMPING * both

        def leftover(p):
            c, acc = nearby(w1, u1, p)
            value = f1[1, p] - diag1[p] * (c - acc)
            if outer + 1 < OUTER:
                f1[2, p, 8 : 8 + by] = value[8 : 8 + by]
            else:
                last[p - H1] = value[8 : 8 + by]

        loop(H1, H1 + bx, leftover, 4)
        drain(copies1)
        drain(copies2)
        for o in range(1, gy_size):
            along_y(o).wait_send()
        for o in range(1, nx):
            along_x(o).wait_send()

    outs = [
        remote(u1.at[own_x, own_y, their_z], sol_ref.at[mine_x], out_send.at[0], out_recv.at[0], partner, gy),
        remote(last.at[:, :, their_z], res_ref.at[mine_x], out_send.at[1], out_recv.at[1], partner, gy),
    ]
    for copy in outs:
        copy.start()
    sol_ref[mine_x] = u1[own_x, own_y, mine_z]
    res_ref[mine_x] = last[:, :, mine_z]
    for copy in outs:
        copy.wait_send()
    remote(u1.at[own_x, own_y, their_z], sol_ref.at[their_x], out_send.at[0], out_recv.at[0], partner, gy).wait_recv()
    remote(last.at[:, :, their_z], res_ref.at[their_x], out_send.at[1], out_recv.at[1], partner, gy).wait_recv()


def solution(mesh):
    gx_size, gy_size = mesh.shape["gx"], mesh.shape["gy"]

    def on_device(right_side, coefficient):
        full_x, by, half_z = right_side.shape
        bx = full_x // 2
        nx = 2 * gx_size
        lanes = half_z
        p1, r1, l1 = bx + 2 * H1, by + 16, 2 * half_z
        b2, y2 = bx // 2, by // 2
        p2, r2 = 5 * b2, y2 + 16
        p3, r3 = nx * bx // 4 + 2, gy_size * by // 4
        p4, r4 = nx * bx // 8 + 2, gy_size * by // 8
        vm = lambda *shape: pltpu.VMEM(shape, F32)
        sem = lambda *shape: pltpu.SemaphoreType.DMA(shape)
        return pl.pallas_call(
            functools.partial(kernel, gx_size, gy_size),
            out_shape=(jax.ShapeDtypeStruct(right_side.shape, F32),) * 2,
            in_specs=[pl.BlockSpec(memory_space=pltpu.HBM)] * 2,
            out_specs=(pl.BlockSpec(memory_space=pltpu.VMEM),) * 2,
            scratch_shapes=[
                vm(3, p1, r1, l1), vm(6, p1, r1, l1), vm(p1, r1, l1), vm(p1, r1, l1), vm(p1, r1, l1),
                vm(FINE_DEGREE, p1, r1, l1), vm(p1, r1, l1), vm(bx, by, l1),
                vm(3, p2, r2, lanes), vm(6, p2, r2, lanes), vm(p2, r2, lanes), vm(p2, r2, lanes),
                vm(FINE_DEGREE, p2, r2, lanes), vm(p2, r2, lanes),
                vm(2, nx, gy_size, 8, lanes),
                vm(2, p3, r3, lanes), vm(6, p3, r3, lanes), vm(p3, r3, lanes), vm(p3, r3, lanes),
                vm(FINE_DEGREE, p3, r3, lanes), vm(p3, r3, lanes),
                vm(2, p4, r4, lanes), vm(6, p4, r4, lanes), vm(p4, r4, lanes), vm(p4, r4, lanes),
                vm(2, p4, r4, lanes), vm(p4, r4, lanes),
                vm(max((p3 - 2) * r3, 2 * b2 * by), lanes), vm(b2 + 2, r1, l1), sem(2),
                sem(2), sem(2), sem(2, 8), sem(2, 8), sem(2, 14), sem(2, 14),
                sem(2, gy_size), sem(2, gy_size), sem(2, nx), sem(2, nx), sem(2), sem(2),
            ],
            compiler_params=pltpu.CompilerParams(
                collective_id=0, has_side_effects=True, vmem_limit_bytes=64 * 1024 * 1024
            ),
        )(right_side, coefficient)

    placed = (P("gx", "gy", "grp"), P("gx", "gy", "grp"))
    return jax.shard_map(on_device, mesh=mesh, in_specs=placed, out_specs=placed, check_vma=False)
```
